128 devices in a mesh: store: 16 (over x, z), head: 8 (over y, core).
Axes of the slice: x: 4, y: 4, z: 4, core: 2. Of those that a mesh axis runs over, the one named last changes fastest.
Arguments:
- tile_inputs: bfloat16 [32, 256, 12288], P('store'), may hold values from -6 to 6
- tile_queries: bfloat16 [32, 256, 12288], P('store', 'head'), may hold values from -22 to 22
- key_weight: bfloat16 [12288, 1024], P('store', 'head'), may hold values from -0.0546875 to 0.0546875
- value_weight: bfloat16 [12288, 1024], P('store', 'head'), may hold values from -0.0546875 to 0.0546875
- span_keys: bfloat16 [256, 8, 512, 128], P('store', 'head'), may hold values from -6 to 6
- span_values: bfloat16 [256, 8, 512, 128], P('store', 'head'), may hold values from -6 to 6
- span_slot: int32 [256], replicated, may hold values from 0 to 255, as said below
- retrieval: int32 [32, 8], P('store'), may hold values from 0 to 255, as said below
- tile_ids: int32 [32, 2], P('store'), may hold values from 0 to 31, as said below
Outputs:
- attended: bfloat16 [32, 256, 12288], P('store', 'head')
The draws below stay inside these ranges and needn't reach their ends.
Inputs may be any that keep to these rules, and one draw needn't show every extreme that they name: A permutation: span id c is held at row span_slot[c] of the store, on store device span_slot[c] // 16. `retrieval`: the 8 spans of one query lie on 8 different store devices. Among the spans named by the 2 queries of one store device, at most 1 lie on any one store device, and exactly 1 on some one. `tile_ids`: the 2 tiles of one query are distinct.
All inputs are finite; a program needn't handle non-finite values.
Results may differ from the reference program's by a relative error of at most 0.0068.
Values may be sent and summed in bfloat16 or wider, within the bound.
No kernel may reach another device: no remote copies, remote signals or barrier semaphores. Data moves between devices by JAX's collectives and lax.ppermute only.
A program may use at most 192 MiB of HBM per device.

```python
import jax
import jax.numpy as jnp
from jax import lax

D = 12288
H = 96
KVH = 8
HD = 128
SLOTS = 8
SPAN_LEN = 512
TILE = 128
R = 2
Q_DEV = 2
CH_DEV = 16
QUERIES = 32
SPANS = 256
TILES = 32


def store_layout(key):
    owner_count = SPANS // CH_DEV
    device_count = QUERIES // Q_DEV
    streams = jax.random.split(jax.random.fold_in(key, 501), 6)
    span_rows = jax.random.permutation(streams[0], SPANS).astype(jnp.int32)
    span_at_row = jnp.argsort(span_rows).astype(jnp.int32)
    hot_owner = (jax.random.randint(streams[1], (owner_count,), 0, 4) == 0).astype(jnp.int32)
    liking = jax.random.randint(streams[2], (device_count, owner_count), 0, 64) + 64 * hot_owner[None, :]
    liking = liking * owner_count + jnp.arange(owner_count, dtype=jnp.int32)[None, :]
    preference = jnp.argsort(-liking, axis=1).astype(jnp.int32)
    starts = jax.random.randint(streams[3], (device_count,), 0, owner_count)
    query_steps = jnp.arange(Q_DEV, dtype=jnp.int32)[None, :, None] * SLOTS
    slot_steps = jnp.arange(SLOTS, dtype=jnp.int32)[None, None, :]
    window = (starts[:, None, None] + query_steps + slot_steps) % owner_count
    spread = jnp.broadcast_to(preference[:, None, :], (device_count, Q_DEV, owner_count))
    owner_pick = jnp.take_along_axis(spread, window, axis=2)
    local_first = jax.random.randint(streams[4], (device_count, Q_DEV, SLOTS), 0, CH_DEV)
    local_second = jax.random.randint(streams[5], (device_count, Q_DEV, SLOTS), 0, CH_DEV)
    store_row = owner_pick * CH_DEV + jnp.minimum(local_first, local_second)
    lists = span_at_row[store_row].reshape(QUERIES, SLOTS).astype(jnp.int32)
    return (span_rows, lists)


def draw_span_slot(key, part):
    shared = store_layout(key)
    return shared[0]


def draw_retrieval(key, part):
    shared = store_layout(key)
    return shared[1]


def draw_tile_ids(key, part):
    key = jax.random.fold_in(key, 3)
    order_scores = jax.random.randint(key, (QUERIES, TILES), 0, 1 << 20) * TILES
    order_scores = order_scores + jnp.arange(TILES, dtype=jnp.int32)[None, :]
    return jnp.argsort(order_scores, axis=1)[:, :R].astype(jnp.int32)


def draw_span_keys(key, part):
    key = jax.random.fold_in(key, 5)
    shape = (SPANS, KVH, SPAN_LEN, HD)
    return jnp.clip(jax.random.normal(key, shape, jnp.float32), -6.0, 6.0).astype(jnp.bfloat16)


def draw_tile_queries(key, part):
    key = jax.random.fold_in(key, 7)
    shape = (QUERIES, R * TILE, H * HD)
    return jnp.clip(2.0 * jax.random.normal(key, shape, jnp.float32), -12.0, 12.0).astype(jnp.bfloat16)


def steps_of(own_key, extent, shards, least, high):
    level = 1.0
    for axis_at, blocks in shards:
        steps = jax.random.uniform(jax.random.fold_in(jax.random.fold_in(own_key, 6), axis_at), (blocks,), jnp.float32, least / len(shards), high / len(shards))
        level = level * jnp.repeat(jnp.exp(steps), extent[axis_at] // blocks).reshape((-1,) + (1,) * (len(extent) - 1 - axis_at))
    return level


def gaussian(key, extent, width, reach, cuts=(), kind=jnp.bfloat16):
    level = steps_of(key, extent, cuts, -0.22, 0.18) if cuts else 1.0
    drawn = jax.random.normal(key, extent, jnp.float32) * width * level
    return jnp.minimum(jnp.maximum(drawn, -reach), reach).astype(kind)


def setup_inputs(seed: int = 0) -> dict:
    key_list = jax.random.split(jax.random.key(seed), 10)
    tile_inputs = gaussian(key_list[0], (QUERIES, R * TILE, D), 1.0, 6.0, ((0, 16),))
    tile_queries = draw_tile_queries(jax.random.fold_in(key_list[9], 71), 0)
    key_weight = gaussian(key_list[2], (D, KVH * HD), D ** -0.5, 0.0546875, ((0, 16), (1, 8)))
    value_weight = gaussian(key_list[3], (D, KVH * HD), D ** -0.5, 0.0546875, ((0, 16), (1, 8)))
    span_keys = draw_span_keys(jax.random.fold_in(key_list[9], 71), 0)
    span_values = gaussian(key_list[5], (SPANS, KVH, SPAN_LEN, HD), 1.0, 6.0, ((0, 16), (1, 8)))
    span_slot = draw_span_slot(jax.random.fold_in(key_list[9], 71), 0)
    retrieval = draw_retrieval(jax.random.fold_in(key_list[9], 71), 0)
    tile_ids = draw_tile_ids(jax.random.fold_in(key_list[9], 71), 0)
    return {"tile_inputs": tile_inputs, "tile_queries": tile_queries, "key_weight": key_weight, "value_weight": value_weight, "span_keys": span_keys, "span_values": span_values, "span_slot": span_slot, "retrieval": retrieval, "tile_ids": tile_ids}


rope_base = 1000000.0


def rotate(block_values, positions):
    half_width = block_values.shape[-1] // 2
    exponent = jnp.arange(half_width, dtype=jnp.float32) * (2.0 / block_values.shape[-1])
    frequency = jnp.power(jnp.float32(rope_base), -exponent)
    angle = positions.astype(jnp.float32)[..., None] * frequency
    cosine = jnp.cos(angle)
    sine = jnp.sin(angle)
    leading = block_values[..., :half_width]
    trailing = block_values[..., half_width:]
    return jnp.concatenate([leading * cosine - trailing * sine, trailing * cosine + leading * sine], axis=-1)


def tile_positions(tile_list, tile_len):
    offsets = jnp.arange(tile_len, dtype=jnp.int32)
    return (tile_list.astype(jnp.int32)[:, None] * tile_len + offsets[None, :]).reshape(-1)


def reference(tile_inputs, tile_queries, key_weight, value_weight, span_keys, span_values, span_slot, retrieval, tile_ids):
    kv_heads = span_keys.shape[1]
    span_len = span_keys.shape[2]
    head_dim = span_keys.shape[3]
    tile_rows = tile_inputs.shape[1]
    tile_len = tile_rows // tile_ids.shape[1]
    score_scale = head_dim ** -0.5
    offsets = (jnp.arange(SLOTS, dtype=jnp.int32) * span_len)[:, None, None]
    key_positions = jnp.arange(SLOTS * span_len, dtype=jnp.int32)

    def one_query(query_item):
        inputs_one, queries_one, lists_one, tiles_one = query_item
        store_rows = span_slot[lists_one]
        stored_keys = rotate(span_keys[store_rows].astype(jnp.float32), offsets).astype(jnp.bfloat16)
        key_block = stored_keys.transpose(1, 0, 2, 3).reshape(kv_heads, SLOTS * span_len, head_dim)
        value_block = span_values[store_rows].transpose(1, 0, 2, 3).reshape(kv_heads, SLOTS * span_len, head_dim)
        positions = tile_positions(tiles_one, tile_len)
        fresh_keys = jnp.dot(inputs_one, key_weight, preferred_element_type=jnp.float32).reshape(tile_rows, kv_heads, head_dim)
        fresh_keys = rotate(fresh_keys, positions[:, None]).astype(jnp.bfloat16).transpose(1, 0, 2)
        fresh_values = jnp.dot(inputs_one, value_weight, preferred_element_type=jnp.float32).astype(jnp.bfloat16)
        fresh_values = fresh_values.reshape(tile_rows, kv_heads, head_dim).transpose(1, 0, 2)
        anchor = jnp.zeros((), jnp.int32)
        for tile_number in range(tiles_one.shape[0]):
            start = (tiles_one[tile_number] * tile_len).astype(jnp.int32)
            lower = tile_number * tile_len
            key_block = lax.dynamic_update_slice(key_block, fresh_keys[:, lower:lower + tile_len], (anchor, start, anchor))
            value_block = lax.dynamic_update_slice(value_block, fresh_values[:, lower:lower + tile_len], (anchor, start, anchor))
        grouped = queries_one.reshape(tile_rows, kv_heads, -1, head_dim).transpose(1, 0, 2, 3)
        allowed = key_positions[None, :] <= positions[:, None]

        def one_head(head_item):
            query_head, key_head, value_head = head_item
            scores = jnp.einsum("rgd,sd->grs", query_head.astype(jnp.float32), key_head.astype(jnp.float32)) * score_scale
            scores = jnp.where(allowed[None], scores, -1e30)
            row_max = jnp.max(scores, axis=-1, keepdims=True)
            weights = jnp.exp(scores - row_max)
            row_total = jnp.sum(weights, axis=-1)
            rounded = weights.astype(jnp.bfloat16)
            mixed_sum = jnp.einsum("grs,sd->rgd", rounded.astype(jnp.float32), value_head.astype(jnp.float32))
            return (mixed_sum / row_total.T[:, :, None]).astype(jnp.bfloat16)

        head_outputs = lax.map(one_head, (grouped, key_block, value_block))
        return head_outputs.transpose(1, 0, 2, 3).reshape(tile_rows, -1)

    return lax.map(one_query, (tile_inputs, tile_queries, retrieval, tile_ids))
```

```python
import functools
import math

import jax
import jax.numpy as jnp
from jax import lax
from jax.experimental import pallas as pl
from jax.experimental.pallas import tpu as pltpu
from jax.sharding import PartitionSpec as P

rope_base = 1000000.0
low = -1e30


def rope_tables(positions, width):
    half_width = width // 2
    exponent = jnp.arange(half_width, dtype=jnp.float32) * (2.0 / width)
    frequency = jnp.power(jnp.float32(rope_base), -exponent)
    angle = positions.astype(jnp.float32)[..., None] * frequency
    cosine = jnp.cos(angle)
    sine = jnp.sin(angle)
    return (
        jnp.concatenate([cosine, cosine], axis=-1),
        jnp.concatenate([-sine, sine], axis=-1),
    )


def rotate(values, cosine, signed_sine):
    swapped = pltpu.roll(values, values.shape[-1] // 2, 1)
    return values * cosine + swapped * signed_sine


def whole(shape):
    return pl.BlockSpec(shape, lambda *_: (0,) * len(shape))


def split_kernel(x_ref, o_ref):
    o_ref[0] = x_ref[...]


def split_columns(x, pieces):
    lead, rows, width = x.shape
    part = width // pieces
    return pl.pallas_call(
        split_kernel,
        grid=(pieces,),
        in_specs=[pl.BlockSpec((lead, rows, part), lambda j: (0, 0, j))],
        out_specs=pl.BlockSpec((1, lead, rows, part), lambda j: (j, 0, 0, 0)),
        out_shape=jax.ShapeDtypeStruct((pieces, lead, rows, part), x.dtype),
        name="split_columns",
    )(x)


def join_kernel(x_ref, o_ref):
    o_ref[...] = x_ref[0]


def join_columns(x):
    pieces, lead, rows, part = x.shape
    return pl.pallas_call(
        join_kernel,
        grid=(pieces,),
        in_specs=[pl.BlockSpec((1, lead, rows, part), lambda j: (j, 0, 0, 0))],
        out_specs=pl.BlockSpec((lead, rows, part), lambda j: (0, 0, j)),
        out_shape=jax.ShapeDtypeStruct((lead, rows, pieces * part), x.dtype),
        name="join_columns",
    )(x)


def pick_kernel(rows_ref, keys_ref, values_ref, o_ref, sems):
    count = o_ref.shape[0]
    copies = []
    for d in range(count):
        row = rows_ref[d]
        copies.append(pltpu.make_async_copy(keys_ref.at[row, 0], o_ref.at[d, 0], sems.at[d, 0]))
        copies.append(pltpu.make_async_copy(values_ref.at[row, 0], o_ref.at[d, 1], sems.at[d, 1]))
    for copy in copies:
        copy.start()
    for copy in copies:
        copy.wait()


def pick_spans(rows, keys, values):
    count = rows.shape[0]
    span_len, head_dim = keys.shape[2:]
    return pl.pallas_call(
        pick_kernel,
        in_specs=[
            pl.BlockSpec(memory_space=pltpu.SMEM),
            pl.BlockSpec(memory_space=pl.ANY),
            pl.BlockSpec(memory_space=pl.ANY),
        ],
        out_specs=pl.BlockSpec(memory_space=pl.ANY),
        out_shape=jax.ShapeDtypeStruct((count, 2, span_len, head_dim), keys.dtype),
        scratch_shapes=[pltpu.SemaphoreType.DMA((count, 2))],
        name="pick_spans",
    )(rows, keys, values)


def head_rows(q_ref, head_dim):
    tile = q_ref[...].reshape(-1, q_ref.shape[-1])
    heads = tile.shape[-1] // head_dim
    return [tile[:, g * head_dim : (g + 1) * head_dim] for g in range(heads)]


def stored_kernel(
    exp_scale, owner_ref, tile_ref, q_ref, got_ref, cos_ref, sin_ref, acc_ref, stat_ref, q_all, m_all, acc_all
):
    query = pl.program_id(0)
    number = pl.program_id(1)
    span_len, head_dim = got_ref.shape[2:]
    own = tile_ref[query, number]
    other = tile_ref[query, 1 - number]
    tile_len = q_ref.shape[0] * q_ref.shape[2]
    pair = 2 * tile_len
    per_span = span_len // tile_len
    lane = lax.broadcasted_iota(jnp.int32, (tile_len, head_dim), 1)
    marker = (lane == 0).astype(jnp.bfloat16)
    for g, part in enumerate(head_rows(q_ref, head_dim)):
        q_all[g * tile_len : (g + 1) * tile_len, :head_dim] = part
        q_all[g * tile_len : (g + 1) * tile_len, head_dim:] = marker
    m_all[...] = jnp.full_like(m_all, low)
    acc_all[...] = jnp.zeros_like(acc_all)
    key_lane = lax.broadcasted_iota(jnp.int32, (span_len, head_dim), 1)
    key_row = lax.broadcasted_iota(jnp.int32, (span_len, head_dim), 0)
    ones = jnp.ones((span_len, head_dim), jnp.bfloat16)

    def step(p, carry):
        owner = owner_ref[query, p]
        keys = rotate(
            got_ref[owner, 0].astype(jnp.float32), cos_ref[pl.ds(p, 1), :], sin_ref[pl.ds(p, 1), :]
        ).astype(jnp.bfloat16)
        key_tile = p * per_span + key_row // tile_len
        hidden = (key_lane == 0) & ((key_tile >= own) | (key_tile == other))
        keys = jnp.concatenate([keys, jnp.where(hidden, low, 0.0).astype(jnp.bfloat16)], axis=1)
        values = jnp.concatenate([got_ref[owner, 1], ones], axis=1)
        for start in range(0, q_all.shape[0], pair):
            at = pl.ds(start, pair)
            scores = lax.dot_general(
                q_all[at, :], keys, (((1,), (1,)), ((), ())), preferred_element_type=jnp.float32
            )
            before = m_all[at, :]
            after = jnp.maximum(before, jnp.max(scores, axis=1, keepdims=True))
            weights = jnp.exp2((scores - after[:, :1]) * exp_scale)
            fade = jnp.exp2((before - after) * exp_scale)
            acc_all[at, :] = acc_all[at, :] * fade[:, :1] + jnp.dot(
                weights.astype(jnp.bfloat16), values, preferred_element_type=jnp.float32
            )
            m_all[at, :] = after
        return carry

    lax.fori_loop(0, (own + per_span - 1) // per_span, step, 0)
    acc_ref[0, 0] = acc_all[:, :head_dim]
    wide = lax.broadcasted_iota(jnp.int32, m_all.shape, 1)
    stat_ref[0, 0] = jnp.where(wide < head_dim // 2, m_all[...], acc_all[:, head_dim:])


def stored_attention(owner, tile_ids, queries, got, cosine, signed_sine, exp_scale):
    sources, queries_dev, rows, part = queries.shape
    recompute = tile_ids.shape[1]
    head_dim = got.shape[3]
    per_tile = sources // recompute
    tile_len = per_tile * rows
    all_rows = tile_len * (part // head_dim)
    state = jax.ShapeDtypeStruct((queries_dev, recompute, all_rows, head_dim), jnp.float32)
    state_spec = pl.BlockSpec((1, 1, all_rows, head_dim), lambda i, j, *_: (i, j, 0, 0))
    return pl.pallas_call(
        functools.partial(stored_kernel, exp_scale),
        grid_spec=pltpu.PrefetchScalarGridSpec(
            num_scalar_prefetch=2,
            grid=(queries_dev, recompute),
            in_specs=[
                pl.BlockSpec((per_tile, 1, rows, part), lambda i, j, *_: (j, i, 0, 0)),
                whole(got.shape),
                whole(cosine.shape),
                whole(signed_sine.shape),
            ],
            out_specs=[state_spec, state_spec],
            scratch_shapes=[
                pltpu.VMEM((all_rows, 2 * head_dim), jnp.bfloat16),
                pltpu.VMEM((all_rows, head_dim), jnp.float32),
                pltpu.VMEM((all_rows, 2 * head_dim), jnp.float32),
            ],
        ),
        out_shape=[state, state],
        compiler_params=pltpu.CompilerParams(vmem_limit_bytes=48 * 2**20),
        cost_estimate=pl.CostEstimate(
            flops=8 * 10**9, bytes_accessed=15 * 10**6, transcendentals=16 * 10**6
        ),
        name="stored_attention",
    )(owner, tile_ids, queries, got, cosine, signed_sine)


def project_kernel(x_ref, w_ref, cos_ref, sin_ref, keys_ref, values_ref, total):
    step = pl.program_id(0)
    head_dim = keys_ref.shape[1]

    @pl.when(step == 0)
    def _():
        total[...] = jnp.zeros_like(total)

    total[...] += jnp.dot(x_ref[...], w_ref[...], preferred_element_type=jnp.float32)

    @pl.when(step == pl.num_programs(0) - 1)
    def _():
        keys_ref[...] = rotate(total[:, :head_dim], cos_ref[...], sin_ref[...]).astype(jnp.bfloat16)
        values_ref[...] = total[:, head_dim:].astype(jnp.bfloat16)


def project(x, weights, cosine, signed_sine):
    rows, width = x.shape
    columns = weights.shape[1]
    head_dim = columns // 2
    depth = 1536
    out = jax.ShapeDtypeStruct((rows, head_dim), jnp.bfloat16)
    return pl.pallas_call(
        project_kernel,
        grid=(width // depth,),
        in_specs=[
            pl.BlockSpec((rows, depth), lambda k: (0, k)),
            pl.BlockSpec((depth, columns), lambda k: (k, 0)),
            whole(cosine.shape),
            whole(signed_sine.shape),
        ],
        out_specs=[whole(out.shape), whole(out.shape)],
        out_shape=[out, out],
        scratch_shapes=[pltpu.VMEM((rows, columns), jnp.float32)],
        compiler_params=pltpu.CompilerParams(vmem_limit_bytes=48 * 2**20),
        cost_estimate=pl.CostEstimate(
            flops=2 * rows * width * columns, bytes_accessed=2 * width * (rows + columns), transcendentals=0
        ),
        name="project",
    )(x, weights, cosine, signed_sine)


def fresh_kernel(exp_scale, tile_ref, q_ref, keys_ref, values_ref, acc_ref, stat_ref, o_ref):
    query = pl.program_id(0)
    number = pl.program_id(1)
    rows, head_dim = keys_ref.shape
    tile_len = rows // 2
    own = tile_ref[query, number]
    other = tile_ref[query, 1 - number]
    row = lax.broadcasted_iota(jnp.int32, (tile_len, rows), 0)
    column = lax.broadcasted_iota(jnp.int32, (tile_len, rows), 1)
    in_own = column // tile_len == number
    allowed = (in_own & (column % tile_len <= row)) | (jnp.logical_not(in_own) & (other < own))
    bias = jnp.where(allowed, 0.0, low)
    keys = keys_ref[...]
    values = jnp.concatenate([values_ref[...], jnp.ones((rows, head_dim), jnp.bfloat16)], axis=1)
    half = head_dim // 2
    for g, part in enumerate(head_rows(q_ref, head_dim)):
        at = pl.ds(g * tile_len, tile_len)
        scores = lax.dot_general(
            part, keys, (((1,), (1,)), ((), ())), preferred_element_type=jnp.float32
        )
        scores = scores + bias
        stat = stat_ref[0, 0, at, :]
        before = stat[:, :1]
        after = jnp.maximum(before, jnp.max(scores, axis=1, keepdims=True))
        weights = jnp.exp2((scores - after) * exp_scale)
        fade = jnp.exp2((before - after) * exp_scale)
        mixed = jnp.dot(weights.astype(jnp.bfloat16), values, preferred_element_type=jnp.float32)
        total = stat[:, half : half + 1] * fade + mixed[:, head_dim : head_dim + 1]
        result = (acc_ref[0, 0, at, :] * fade + mixed[:, :head_dim]) / total
        o_ref[:, 0, :, g * head_dim : (g + 1) * head_dim] = result.astype(jnp.bfloat16).reshape(
            o_ref.shape[0], o_ref.shape[2], head_dim
        )


def fresh_attention(tile_ids, queries, keys, values, acc, stat, exp_scale):
    sources, queries_dev, rows, part = queries.shape
    recompute = tile_ids.shape[1]
    head_dim = keys.shape[1]
    per_tile = sources // recompute
    tile_rows = keys.shape[0] // queries_dev
    q_spec = pl.BlockSpec((per_tile, 1, rows, part), lambda i, j, *_: (j, i, 0, 0))
    key_spec = pl.BlockSpec((tile_rows, head_dim), lambda i, j, *_: (i, 0))
    state_spec = pl.BlockSpec((1, 1) + acc.shape[2:], lambda i, j, *_: (i, j, 0, 0))
    return pl.pallas_call(
        functools.partial(fresh_kernel, exp_scale),
        grid_spec=pltpu.PrefetchScalarGridSpec(
            num_scalar_prefetch=1,
            grid=(queries_dev, recompute),
            in_specs=[q_spec, key_spec, key_spec, state_spec, state_spec],
            out_specs=q_spec,
        ),
        out_shape=jax.ShapeDtypeStruct(queries.shape, queries.dtype),
        compiler_params=pltpu.CompilerParams(vmem_limit_bytes=48 * 2**20),
        cost_estimate=pl.CostEstimate(
            flops=10**9, bytes_accessed=10 * 10**6, transcendentals=2 * 10**6
        ),
        name="fresh_attention",
    )(tile_ids, queries, keys, values, acc, stat)


def body(
    tile_inputs,
    tile_queries,
    key_weight,
    value_weight,
    span_keys,
    span_values,
    span_slot,
    retrieval,
    tile_ids,
):
    queries_dev, tile_rows, width = tile_inputs.shape
    per_store, _, span_len, head_dim = span_keys.shape
    slot_count = retrieval.shape[1]
    recompute = tile_ids.shape[1]
    tile_len = tile_rows // recompute
    store_count = lax.axis_size("store")
    head_count = lax.axis_size("head")
    exp_scale = head_dim ** (-0.5) * math.log2(math.e)

    weights = lax.all_gather(
        jnp.concatenate([key_weight, value_weight], axis=1), "store", axis=0, tiled=True
    )

    store_rows = span_slot[retrieval]
    owners = store_rows // per_store
    hit = owners.reshape(1, -1) == jnp.arange(store_count, dtype=jnp.int32)[:, None]
    wanted = jnp.max(jnp.where(hit, (store_rows % per_store).reshape(1, -1), 0), axis=1)
    incoming = lax.all_to_all(
        wanted.reshape(store_count, 1), "store", split_axis=0, concat_axis=0, tiled=True
    )
    picked = pick_spans(incoming.reshape(-1), span_keys, span_values)
    got = lax.all_to_all(picked, "store", split_axis=0, concat_axis=0, tiled=True)

    queries = lax.all_to_all(
        split_columns(tile_queries, head_count), "head", split_axis=0, concat_axis=0, tiled=True
    )

    offsets = jnp.arange(tile_len, dtype=jnp.int32)
    positions = (tile_ids[:, :, None] * tile_len + offsets).reshape(-1)
    fresh_cos, fresh_sin = rope_tables(positions, head_dim)
    slot_cos, slot_sin = rope_tables(jnp.arange(slot_count, dtype=jnp.int32) * span_len, head_dim)

    acc, stat = stored_attention(owners, tile_ids, queries, got, slot_cos, slot_sin, exp_scale)
    fresh_keys, fresh_values = project(
        tile_inputs.reshape(queries_dev * tile_rows, width), weights, fresh_cos, fresh_sin
    )
    mixed = fresh_attention(tile_ids, queries, fresh_keys, fresh_values, acc, stat, exp_scale)
    return join_columns(
        lax.all_to_all(mixed, "head", split_axis=0, concat_axis=0, tiled=True)
    )


def solution(mesh):
    placed = (
        P("store", None, None),
        P("store", "head", None),
        P("store", "head"),
        P("store", "head"),
        P("store", "head", None, None),
        P("store", "head", None, None),
        P(),
        P("store", None),
        P("store", None),
    )
    return jax.shard_map(
        body, mesh=mesh, in_specs=placed, out_specs=P("store", "head", None), check_vma=False
    )
```

```python
import functools
import math

import jax
import jax.numpy as jnp
from jax import lax
from jax.experimental import pallas as pl
from jax.experimental.pallas import tpu as pltpu
from jax.sharding import PartitionSpec as P

rope_base = 1000000.0
low = -1e30


def rope_tables(positions, width):
    half_width = width // 2
    exponent = jnp.arange(half_width, dtype=jnp.float32) * (2.0 / width)
    frequency = jnp.power(jnp.float32(rope_base), -exponent)
    angle = positions.astype(jnp.float32)[..., None] * frequency
    cosine = jnp.cos(angle)
    sine = jnp.sin(angle)
    return (
        jnp.concatenate([cosine, cosine], axis=-1),
        jnp.concatenate([-sine, sine], axis=-1),
    )


def rotate(values, cosine, signed_sine):
    swapped = pltpu.roll(values, values.shape[-1] // 2, 1)
    return values * cosine + swapped * signed_sine


def whole(shape):
    return pl.BlockSpec(shape, lambda *_: (0,) * len(shape))


def head_partner(me, step, count, sign):
    ring = count // 2
    turn = lax.rem(me // 2 + sign * (step // 2) + ring, ring)
    return 2 * turn + lax.rem(lax.rem(me, 2) + lax.rem(step, 2), 2)


def split_kernel(x_ref, *o_refs):
    me = lax.axis_index("head")
    part = o_refs[0].shape[2]
    for step, o_ref in enumerate(o_refs):
        to = head_partner(me, step, len(o_refs), 1)
        o_ref[...] = x_ref[:, :, pl.ds(pl.multiple_of(to * part, part), part)]


def split_columns(x, pieces):
    lead, rows, width = x.shape
    out = jax.ShapeDtypeStruct((lead, rows, width // pieces), x.dtype)
    return pl.pallas_call(split_kernel, out_shape=[out] * pieces, name="split_columns")(x)


def assemble_kernel(*refs):
    pieces = refs[:-2]
    o_ref, staged = refs[-2:]
    me = lax.axis_index("head")
    for step, piece in enumerate(pieces):
        staged[head_partner(me, step, len(pieces), -1)] = piece[...]
    queries_dev, recompute, double, all_rows = o_ref.shape
    head_dim = double // 2
    sources, _, rows, part = staged.shape
    per_tile = sources // recompute
    tile_len = per_tile * rows
    marker = (lax.broadcasted_iota(jnp.int32, (head_dim, all_rows), 0) == 0).astype(jnp.bfloat16)
    for i in range(queries_dev):
        for j in range(recompute):
            tile = staged[j * per_tile : (j + 1) * per_tile, i].reshape(tile_len, part)
            for g in range(part // head_dim):
                o_ref[i, j, :head_dim, g * tile_len : (g + 1) * tile_len] = tile[
                    :, g * head_dim : (g + 1) * head_dim
                ].T
            o_ref[i, j, head_dim:, :] = marker


def assemble(pieces, recompute, head_dim):
    queries_dev, rows, part = pieces[0].shape
    all_rows = len(pieces) // recompute * rows * (part // head_dim)
    return pl.pallas_call(
        assemble_kernel,
        out_shape=jax.ShapeDtypeStruct((queries_dev, recompute, 2 * head_dim, all_rows), pieces[0].dtype),
        scratch_shapes=[pltpu.VMEM((len(pieces),) + pieces[0].shape, pieces[0].dtype)],
        compiler_params=pltpu.CompilerParams(vmem_limit_bytes=20 * 2**20),
        name="assemble",
    )(*pieces)


def join_kernel(x_ref, o_ref):
    part = x_ref.shape[3]
    for j in range(x_ref.shape[0]):
        o_ref[:, :, j * part : (j + 1) * part] = x_ref[j]


def join_columns(x):
    pieces, lead, rows, part = x.shape
    return pl.pallas_call(
        join_kernel,
        out_shape=jax.ShapeDtypeStruct((lead, rows, pieces * part), x.dtype),
        name="join_columns",
    )(x)


def pick_kernel(rows_ref, keys_ref, values_ref, *o_refs):
    def step(d, carry):
        row = rows_ref[d]
        start = 0
        for o_ref in o_refs:
            at = slice(start, start + o_ref.shape[2])
            o_ref[d, 0] = keys_ref[row, 0, at]
            o_ref[d, 1] = values_ref[row, 0, at]
            start = at.stop
        return carry

    lax.fori_loop(0, o_refs[0].shape[0], step, 0)


def pick_spans(rows, keys, values, pieces):
    count = rows.shape[0]
    span_len, head_dim = keys.shape[2:]
    out = jax.ShapeDtypeStruct((count, 2, span_len // pieces, head_dim), keys.dtype)
    return pl.pallas_call(
        pick_kernel,
        in_specs=[
            pl.BlockSpec(memory_space=pltpu.SMEM),
            pl.BlockSpec(memory_space=pltpu.VMEM),
            pl.BlockSpec(memory_space=pltpu.VMEM),
        ],
        out_specs=[pl.BlockSpec(memory_space=pltpu.VMEM)] * pieces,
        out_shape=[out] * pieces,
        compiler_params=pltpu.CompilerParams(vmem_limit_bytes=20 * 2**20),
        name="pick_spans",
    )(rows, keys, values)


def blend(scores, before, exp_scale):
    after = jnp.maximum(before, jnp.max(scores, axis=0, keepdims=True))
    weights = jnp.exp2((scores - after) * exp_scale).astype(jnp.bfloat16)
    fade = jnp.exp2((before - after) * exp_scale)
    return after, weights, fade


def add_keys(exp_scale, q_ref, acc_ref, top_ref, keys, values, bias, wide):
    all_rows = q_ref.shape[3]
    depth = keys.shape[1]
    ones = jnp.ones((acc_ref.shape[2] - values.shape[1], keys.shape[0]), jnp.bfloat16)
    values = jnp.concatenate([values.T, ones], axis=0)
    blocks = [pl.ds(start, wide) for start in range(0, all_rows, wide)]
    scores = {}
    for turn in range(-1, len(blocks)):
        if turn + 1 < len(blocks):
            scores[turn + 1] = jnp.dot(
                keys, q_ref[0, 0, :depth, blocks[turn + 1]], preferred_element_type=jnp.float32
            )
        if turn >= 0:
            at = blocks[turn]
            now = scores.pop(turn)
            if bias is not None:
                now = now + bias
            after, weights, fade = blend(now, top_ref[0, 0, :1, at], exp_scale)
            top_ref[0, 0, :1, at] = after
            acc_ref[0, 0, :, at] = acc_ref[0, 0, :, at] * fade + jnp.dot(
                values, weights, preferred_element_type=jnp.float32
            )


def attend_kernel(exp_scale, tile_len, piece, pieces, fresh, started, finish, *refs):
    refs = list(refs)
    owner_ref, tile_ref, q_ref = refs[:3]
    del refs[:3]
    query = pl.program_id(0)
    number = pl.program_id(1)
    own = tile_ref[query, number]
    other = tile_ref[query, 1 - number]
    if piece is not None:
        got_ref, cos_ref, sin_ref = refs[:3]
        del refs[:3]
    if fresh:
        keys_ref, values_ref = refs[:2]
        del refs[:2]
    if started:
        acc_in, top_in = refs[:2]
        del refs[:2]
    if finish:
        o_ref = refs.pop(0)
    acc_ref, top_ref = refs
    head_dim = q_ref.shape[2] // 2
    wide = 4 * tile_len
    all_rows = q_ref.shape[3]
    if started:
        acc_ref[...] = acc_in[...]
        top_ref[...] = top_in[...]
    else:
        top_ref[...] = jnp.full_like(top_ref, low)
        acc_ref[...] = jnp.zeros_like(acc_ref)
    if piece is not None:
        part_len = got_ref.shape[2]
        per_part = part_len // tile_len
        per_span = per_part * pieces
        key_lane = lax.broadcasted_iota(jnp.int32, (part_len, head_dim), 1)
        key_row = lax.broadcasted_iota(jnp.int32, (part_len, head_dim), 0)

        def step(group, carry):
            key_parts = []
            value_parts = []
            for inner in range(pieces):
                p = group * pieces + inner
                owner = owner_ref[query, p]
                turned = rotate(
                    got_ref[owner, 0].astype(jnp.float32),
                    cos_ref[pl.ds(p, 1), :],
                    sin_ref[pl.ds(p, 1), :],
                ).astype(jnp.bfloat16)
                key_tile = p * per_span + piece * per_part + key_row // tile_len
                hidden = (key_lane == 0) & ((key_tile >= own) | (key_tile == other))
                key_parts.append(
                    jnp.concatenate(
                        [turned, jnp.where(hidden, low, 0.0).astype(jnp.bfloat16)], axis=1
                    )
                )
                value_parts.append(got_ref[owner, 1])
            keys = jnp.concatenate(key_parts, axis=0)
            values = jnp.concatenate(value_parts, axis=0)
            add_keys(exp_scale, q_ref, acc_ref, top_ref, keys, values, None, wide)
            return carry

        spans = (own - piece * per_part + per_span - 1) // per_span
        lax.fori_loop(0, (spans + pieces - 1) // pieces, step, 0)
    if fresh:
        rows = keys_ref.shape[0]
        key = lax.broadcasted_iota(jnp.int32, (rows, tile_len), 0)
        row = lax.broadcasted_iota(jnp.int32, (rows, tile_len), 1)
        in_own = key // tile_len == number
        allowed = (in_own & (key % tile_len <= row)) | (jnp.logical_not(in_own) & (other < own))
        bias = jnp.concatenate([jnp.where(allowed, 0.0, low)] * (wide // tile_len), axis=1)
        add_keys(exp_scale, q_ref, acc_ref, top_ref, keys_ref[...], values_ref[...], bias, wide)
    if finish:
        for start in range(0, all_rows, wide):
            at = pl.ds(start, wide)
            result = acc_ref[0, 0, :head_dim, at] / acc_ref[0, 0, head_dim : head_dim + 1, at]
            result = result.astype(jnp.bfloat16).T
            for h in range(0, wide, tile_len):
                column = (start + h) // tile_len * head_dim
                o_ref[:, 0, :, column : column + head_dim] = result[h : h + tile_len].reshape(
                    o_ref.shape[0], o_ref.shape[2], head_dim
                )


def attend(owner, tile_ids, queries, exp_scale, tile_len, sources=None, stored=None, piece=None, pieces=1, fresh=None, state=None):
    queries_dev, recompute, double, all_rows = queries.shape
    head_dim = double // 2
    args = [queries]
    specs = [pl.BlockSpec((1, 1, double, all_rows), lambda i, j, *_: (i, j, 0, 0))]
    if stored is not None:
        args += stored
        specs += [whole(x.shape) for x in stored]
    if fresh is not None:
        args += fresh
        specs += [
            pl.BlockSpec((x.shape[0] // queries_dev, head_dim), lambda i, j, *_: (i, 0)) for x in fresh
        ]
    shapes = [(head_dim + 16, all_rows), (8, all_rows)]
    state_specs = [pl.BlockSpec((1, 1) + shape, lambda i, j, *_: (i, j, 0, 0)) for shape in shapes]
    if state is not None:
        args += state
        specs += state_specs
    if sources is None:
        out_shape = [
            jax.ShapeDtypeStruct((queries_dev, recompute) + shape, jnp.float32) for shape in shapes
        ]
        out_specs = state_specs
        scratch = []
    else:
        rows = recompute * tile_len // sources
        part = all_rows // tile_len * head_dim
        out_shape = jax.ShapeDtypeStruct((sources, queries_dev, rows, part), queries.dtype)
        out_specs = pl.BlockSpec((sources // recompute, 1, rows, part), lambda i, j, *_: (j, i, 0, 0))
        scratch = [pltpu.VMEM((1, 1) + shape, jnp.float32) for shape in shapes]
    return pl.pallas_call(
        functools.partial(
            attend_kernel, exp_scale, tile_len, piece, pieces, fresh is not None, state is not None, sources is not None
        ),
        grid_spec=pltpu.PrefetchScalarGridSpec(
            num_scalar_prefetch=2,
            grid=(queries_dev, recompute),
            in_specs=specs,
            out_specs=out_specs,
            scratch_shapes=scratch,
        ),
        out_shape=out_shape,
        compiler_params=pltpu.CompilerParams(vmem_limit_bytes=24 * 2**20),
        cost_estimate=pl.CostEstimate(
            flops=16 * 10**9 // pieces if stored is not None else 10**9,
            bytes_accessed=15 * 10**6 // pieces,
            transcendentals=16 * 10**6 // pieces,
        ),
        name="attend" + ("_stored" if stored is not None else "") + ("_fresh" if fresh is not None else ""),
    )(owner, tile_ids, *args)


def project_kernel(x_ref, w_ref, cos_ref, sin_ref, keys_ref, values_ref, total):
    step = pl.program_id(0)
    head_dim = keys_ref.shape[1]

    @pl.when(step == 0)
    def _():
        total[...] = jnp.zeros_like(total)

    total[...] += jnp.dot(x_ref[...], w_ref[...], preferred_element_type=jnp.float32)

    @pl.when(step == pl.num_programs(0) - 1)
    def _():
        keys_ref[...] = rotate(total[:, :head_dim], cos_ref[...], sin_ref[...]).astype(jnp.bfloat16)
        values_ref[...] = total[:, head_dim:].astype(jnp.bfloat16)


def project(x, weights, cosine, signed_sine):
    rows, width = x.shape
    columns = weights.shape[1]
    head_dim = columns // 2
    depth = 3072
    out = jax.ShapeDtypeStruct((rows, head_dim), jnp.bfloat16)
    return pl.pallas_call(
        project_kernel,
        grid=(width // depth,),
        in_specs=[
            pl.BlockSpec((rows, depth), lambda k: (0, k)),
            pl.BlockSpec((depth, columns), lambda k: (k, 0)),
            whole(cosine.shape),
            whole(signed_sine.shape),
        ],
        out_specs=[whole(out.shape), whole(out.shape)],
        out_shape=[out, out],
        scratch_shapes=[pltpu.VMEM((rows, columns), jnp.float32)],
        compiler_params=pltpu.CompilerParams(vmem_limit_bytes=20 * 2**20),
        cost_estimate=pl.CostEstimate(
            flops=2 * rows * width * columns, bytes_accessed=2 * width * (rows + columns), transcendentals=0
        ),
        name="project",
    )(x, weights, cosine, signed_sine)


def body(
    tile_inputs,
    tile_queries,
    key_weight,
    value_weight,
    span_keys,
    span_values,
    span_slot,
    retrieval,
    tile_ids,
):
    queries_dev, tile_rows, width = tile_inputs.shape
    per_store, _, span_len, head_dim = span_keys.shape
    slot_count = retrieval.shape[1]
    recompute = tile_ids.shape[1]
    tile_len = tile_rows // recompute
    store_count = lax.axis_size("store")
    head_count = lax.axis_size("head")
    exp_scale = head_dim ** (-0.5) * math.log2(math.e)

    store_rows = span_slot[retrieval]
    owners = store_rows // per_store
    hit = owners.reshape(1, -1) == jnp.arange(store_count, dtype=jnp.int32)[:, None]
    wanted = jnp.max(jnp.where(hit, (store_rows % per_store).reshape(1, -1), 0), axis=1)
    incoming = lax.all_to_all(
        wanted.reshape(store_count, 1), "store", split_axis=0, concat_axis=0, tiled=True
    )
    weights = lax.all_gather(
        jnp.concatenate([key_weight, value_weight], axis=1), "store", axis=0, tiled=True
    )
    pieces = 2
    picked = pick_spans(incoming.reshape(-1), span_keys, span_values, pieces)
    split = split_columns(tile_queries, head_count)
    ring = head_count // 2
    received = [split[0]]
    for step in range(1, head_count):
        pairs = [
            (me, 2 * ((me // 2 + step // 2) % ring) + (me + step) % 2) for me in range(head_count)
        ]
        received.append(lax.ppermute(split[step], "head", pairs))
    queries = assemble(received, recompute, head_dim)

    got = []
    for part in picked:
        if got:
            part, queries = lax.optimization_barrier((part, queries))
        got.append(lax.all_to_all(part, "store", split_axis=0, concat_axis=0, tiled=True))

    offsets = jnp.arange(tile_len, dtype=jnp.int32)
    positions = (tile_ids[:, :, None] * tile_len + offsets).reshape(-1)
    fresh_cos, fresh_sin = rope_tables(positions, head_dim)
    slot_cos, slot_sin = rope_tables(jnp.arange(slot_count, dtype=jnp.int32) * span_len, head_dim)

    fresh = project(
        tile_inputs.reshape(queries_dev * tile_rows, width), weights, fresh_cos, fresh_sin
    )
    run = functools.partial(attend, owners, tile_ids, queries, exp_scale, tile_len)
    turn = [slot_cos, slot_sin]
    state = run(stored=[got[0]] + turn, piece=0, pieces=pieces)
    state = run(fresh=fresh, state=state)
    mixed = run(stored=[got[1]] + turn, piece=1, pieces=pieces, state=state, sources=head_count)
    return join_columns(
        lax.all_to_all(mixed, "head", split_axis=0, concat_axis=0, tiled=True)
    )


def solution(mesh):
    placed = (
        P("store", None, None),
        P("store", "head", None),
        P("store", "head"),
        P("store", "head"),
        P("store", "head", None, None),
        P("store", "head", None, None),
        P(),
        P("store", None),
        P("store", None),
    )
    return jax.shard_map(
        body, mesh=mesh, in_specs=placed, out_specs=P("store", "head", None), check_vma=False
    )
```

```python
import functools
import math

import jax
import jax.numpy as jnp
from jax import lax
from jax.experimental import pallas as pl
from jax.experimental.pallas import tpu as pltpu
from jax.sharding import PartitionSpec as P

rope_base = 1000000.0
low = -1e30


def rope_tables(positions, width):
    half_width = width // 2
    exponent = jnp.arange(half_width, dtype=jnp.float32) * (2.0 / width)
    frequency = jnp.power(jnp.float32(rope_base), -exponent)
    angle = positions.astype(jnp.float32)[..., None] * frequency
    cosine = jnp.cos(angle)
    sine = jnp.sin(angle)
    return (
        jnp.concatenate([cosine, cosine], axis=-1),
        jnp.concatenate([-sine, sine], axis=-1),
    )


def rotate(values, cosine, signed_sine):
    swapped = pltpu.roll(values, values.shape[-1] // 2, 1)
    return values * cosine + swapped * signed_sine


def whole(shape):
    return pl.BlockSpec(shape, lambda *_: (0,) * len(shape))


def head_partner(me, step, count, sign):
    ring = count // 2
    turn = lax.rem(me // 2 + sign * (step // 2) + ring, ring)
    return 2 * turn + lax.rem(lax.rem(me, 2) + lax.rem(step, 2), 2)


def split_kernel(x_ref, *o_refs):
    me = lax.axis_index("head")
    part = o_refs[0].shape[2]
    for step, o_ref in enumerate(o_refs):
        to = head_partner(me, step, len(o_refs), 1)
        o_ref[...] = x_ref[:, :, pl.ds(pl.multiple_of(to * part, part), part)]


def split_columns(x, pieces):
    lead, rows, width = x.shape
    out = jax.ShapeDtypeStruct((lead, rows, width // pieces), x.dtype)
    return pl.pallas_call(split_kernel, out_shape=[out] * pieces, name="split_columns")(x)


def assemble_kernel(*refs):
    pieces = refs[:-2]
    o_ref, staged = refs[-2:]
    me = lax.axis_index("head")
    for step, piece in enumerate(pieces):
        staged[head_partner(me, step, len(pieces), -1)] = piece[...]
    queries_dev, recompute, double, all_rows = o_ref.shape
    head_dim = double // 2
    sources, _, rows, part = staged.shape
    per_tile = sources // recompute
    tile_len = per_tile * rows
    marker = (lax.broadcasted_iota(jnp.int32, (head_dim, all_rows), 0) == 0).astype(jnp.bfloat16)
    for i in range(queries_dev):
        for j in range(recompute):
            tile = staged[j * per_tile : (j + 1) * per_tile, i].reshape(tile_len, part)
            for g in range(part // head_dim):
                o_ref[i, j, :head_dim, g * tile_len : (g + 1) * tile_len] = tile[
                    :, g * head_dim : (g + 1) * head_dim
                ].T
            o_ref[i, j, head_dim:, :] = marker


def assemble(pieces, recompute, head_dim):
    queries_dev, rows, part = pieces[0].shape
    all_rows = len(pieces) // recompute * rows * (part // head_dim)
    return pl.pallas_call(
        assemble_kernel,
        out_shape=jax.ShapeDtypeStruct((queries_dev, recompute, 2 * head_dim, all_rows), pieces[0].dtype),
        scratch_shapes=[pltpu.VMEM((len(pieces),) + pieces[0].shape, pieces[0].dtype)],
        compiler_params=pltpu.CompilerParams(vmem_limit_bytes=20 * 2**20),
        name="assemble",
    )(*pieces)


def join_kernel(x_ref, o_ref):
    part = x_ref.shape[3]
    for j in range(x_ref.shape[0]):
        o_ref[:, :, j * part : (j + 1) * part] = x_ref[j]


def join_columns(x):
    pieces, lead, rows, part = x.shape
    return pl.pallas_call(
        join_kernel,
        out_shape=jax.ShapeDtypeStruct((lead, rows, pieces * part), x.dtype),
        name="join_columns",
    )(x)


def pick_kernel(rows_ref, keys_ref, values_ref, *o_refs):
    def step(d, carry):
        row = rows_ref[d]
        start = 0
        for o_ref in o_refs:
            at = slice(start, start + o_ref.shape[2])
            o_ref[d, 0] = keys_ref[row, 0, at]
            o_ref[d, 1] = values_ref[row, 0, at]
            start = at.stop
        return carry

    lax.fori_loop(0, o_refs[0].shape[0], step, 0)


def pick_spans(rows, keys, values, pieces):
    count = rows.shape[0]
    span_len, head_dim = keys.shape[2:]
    out = jax.ShapeDtypeStruct((count, 2, span_len // pieces, head_dim), keys.dtype)
    return pl.pallas_call(
        pick_kernel,
        in_specs=[
            pl.BlockSpec(memory_space=pltpu.SMEM),
            pl.BlockSpec(memory_space=pltpu.VMEM),
            pl.BlockSpec(memory_space=pltpu.VMEM),
        ],
        out_specs=[pl.BlockSpec(memory_space=pltpu.VMEM)] * pieces,
        out_shape=[out] * pieces,
        compiler_params=pltpu.CompilerParams(vmem_limit_bytes=20 * 2**20),
        name="pick_spans",
    )(rows, keys, values)


def blend(scores, before, exp_scale):
    after = jnp.maximum(before, jnp.max(scores, axis=0, keepdims=True))
    weights = jnp.exp2((scores - after) * exp_scale).astype(jnp.bfloat16)
    fade = jnp.exp2((before - after) * exp_scale)
    return after, weights, fade


def add_keys(exp_scale, q_ref, acc_ref, top_ref, where, keys, values, bias, wide):
    i, j = where
    all_rows = q_ref.shape[3]
    depth = keys.shape[1]
    ones = jnp.ones((acc_ref.shape[2] - values.shape[1], keys.shape[0]), jnp.bfloat16)
    values = jnp.concatenate([values.T, ones], axis=0)
    blocks = [pl.ds(start, wide) for start in range(0, all_rows, wide)]
    scores = {}
    for turn in range(-1, len(blocks)):
        if turn + 1 < len(blocks):
            scores[turn + 1] = jnp.dot(
                keys, q_ref[i, j, :depth, blocks[turn + 1]], preferred_element_type=jnp.float32
            )
        if turn >= 0:
            at = blocks[turn]
            now = scores.pop(turn)
            if bias is not None:
                now = now + bias
            after, weights, fade = blend(now, top_ref[i, j, :1, at], exp_scale)
            top_ref[i, j, :1, at] = after
            acc_ref[i, j, :, at] = acc_ref[i, j, :, at] * fade + jnp.dot(
                values, weights, preferred_element_type=jnp.float32
            )


def attend_kernel(exp_scale, tile_len, piece, pieces, last, *refs):
    refs = list(refs)
    owner_ref, tile_ref, q_ref, got_ref, cos_ref, sin_ref = refs[:6]
    del refs[:6]
    if last:
        acc_in, top_in, x_ref, w_ref, fresh_cos_ref, fresh_sin_ref, o_ref = refs[:7]
        del refs[:7]
    else:
        acc_out, top_out = refs[:2]
        del refs[:2]
    q_all, held, acc_ref, top_ref, q_sems, span_sems, state_sems = refs[:7]
    if last:
        x_held, w_held, total, x_sems = refs[7:]
    queries_dev, recompute, double, all_rows = q_all.shape
    slots, _, part_len, head_dim = held.shape[1:]
    wide = 4 * tile_len
    per_part = part_len // tile_len
    per_span = per_part * pieces

    def q_copy(i):
        return pltpu.make_async_copy(q_ref.at[i], q_all.at[i], q_sems.at[i])

    def span_copy(i, p):
        return pltpu.make_async_copy(
            got_ref.at[owner_ref[i, p]], held.at[i, p], span_sems.at[i, p]
        )

    def state_copies(i):
        pairs = [(acc_in, acc_ref), (top_in, top_ref)] if last else [(acc_ref, acc_out), (top_ref, top_out)]
        return [
            pltpu.make_async_copy(a.at[i], b.at[i], state_sems.at[i, k]) for k, (a, b) in enumerate(pairs)
        ]

    for i in range(queries_dev):
        q_copy(i).start()
        for p in range(slots):
            span_copy(i, p).start()
        if last:
            for copy in state_copies(i):
                copy.start()
    if last:
        steps = x_sems.shape[0]
        depth = x_held.shape[1] // steps
        copies = []
        for s in range(steps):
            at = pl.ds(s * depth, depth)
            copies.append(pltpu.make_async_copy(x_ref.at[:, at], x_held.at[:, at], x_sems.at[s, 0]))
            copies.append(pltpu.make_async_copy(w_ref.at[at, :], w_held.at[at, :], x_sems.at[s, 1]))
        for copy in copies:
            copy.start()
    key_lane = lax.broadcasted_iota(jnp.int32, (part_len, head_dim), 1)
    key_row = lax.broadcasted_iota(jnp.int32, (part_len, head_dim), 0)
    for i in range(queries_dev):
        if last:
            for copy in state_copies(i):
                copy.wait()
        else:
            top_ref[i] = jnp.full(top_ref.shape[1:], low, jnp.float32)
            acc_ref[i] = jnp.zeros(acc_ref.shape[1:], jnp.float32)
        q_copy(i).wait()

        def step(n, carry, i=i):
            group = n // recompute
            j = lax.rem(n, recompute)
            own = tile_ref[i, j]
            other = tile_ref[i, recompute - 1 - j]

            @pl.when(j == 0)
            def _():
                for inner in range(pieces):
                    span_copy(i, group * pieces + inner).wait()

            @pl.when(group * pieces * per_span + piece * per_part < own)
            def _():
                key_parts = []
                value_parts = []
                for inner in range(pieces):
                    p = group * pieces + inner
                    turned = rotate(
                        held[i, p, 0].astype(jnp.float32),
                        cos_ref[pl.ds(p, 1), :],
                        sin_ref[pl.ds(p, 1), :],
                    ).astype(jnp.bfloat16)
                    key_tile = p * per_span + piece * per_part + key_row // tile_len
                    hidden = (key_lane == 0) & ((key_tile >= own) | (key_tile == other))
                    key_parts.append(
                        jnp.concatenate(
                            [turned, jnp.where(hidden, low, 0.0).astype(jnp.bfloat16)], axis=1
                        )
                    )
                    value_parts.append(held[i, p, 1])
                add_keys(
                    exp_scale,
                    q_all,
                    acc_ref,
                    top_ref,
                    (i, j),
                    jnp.concatenate(key_parts, axis=0),
                    jnp.concatenate(value_parts, axis=0),
                    None,
                    wide,
                )

            return carry

        lax.fori_loop(0, slots // pieces * recompute, step, 0)
        if not last:
            for copy in state_copies(i):
                copy.start()
    if not last:
        for i in range(queries_dev):
            for copy in state_copies(i):
                copy.wait()
        return
    for copy in copies:
        copy.wait()
    total[...] = jnp.dot(x_held[:, :depth], w_held[:depth, :], preferred_element_type=jnp.float32)
    for s in range(1, steps):
        at = pl.ds(s * depth, depth)
        total[...] += jnp.dot(x_held[:, at], w_held[at, :], preferred_element_type=jnp.float32)
    fresh_keys = rotate(total[:, :head_dim], fresh_cos_ref[...], fresh_sin_ref[...]).astype(jnp.bfloat16)
    fresh_values = total[:, head_dim:].astype(jnp.bfloat16)
    rows = recompute * tile_len
    per_tile = o_ref.shape[0] // recompute
    key = lax.broadcasted_iota(jnp.int32, (rows, tile_len), 0)
    row = lax.broadcasted_iota(jnp.int32, (rows, tile_len), 1)
    for i in range(queries_dev):
        for j in range(recompute):
            own = tile_ref[i, j]
            other = tile_ref[i, recompute - 1 - j]
            in_own = key // tile_len == j
            allowed = (in_own & (key % tile_len <= row)) | (jnp.logical_not(in_own) & (other < own))
            bias = jnp.concatenate([jnp.where(allowed, 0.0, low)] * (wide // tile_len), axis=1)
            at_rows = slice(i * rows, (i + 1) * rows)
            add_keys(
                exp_scale, q_all, acc_ref, top_ref, (i, j), fresh_keys[at_rows], fresh_values[at_rows], bias, wide
            )
            for start in range(0, all_rows, wide):
                at = pl.ds(start, wide)
                result = acc_ref[i, j, :head_dim, at] / acc_ref[i, j, head_dim : head_dim + 1, at]
                result = result.astype(jnp.bfloat16).T
                for h in range(0, wide, tile_len):
                    column = (start + h) // tile_len * head_dim
                    o_ref[j * per_tile : (j + 1) * per_tile, i, :, column : column + head_dim] = result[
                        h : h + tile_len
                    ].reshape(per_tile, o_ref.shape[2], head_dim)


def attend(owner, tile_ids, queries, got, turn, exp_scale, tile_len, sources, piece, pieces, state=None, fresh=None):
    queries_dev, recompute, double, all_rows = queries.shape
    head_dim = double // 2
    slots = owner.shape[1]
    last = state is not None
    vmem = pl.BlockSpec(memory_space=pltpu.VMEM)
    smem = pl.BlockSpec(memory_space=pltpu.SMEM)
    hbm = pl.BlockSpec(memory_space=pltpu.HBM)
    shapes = [
        (queries_dev, recompute, head_dim + 16, all_rows),
        (queries_dev, recompute, 8, all_rows),
    ]
    args = [owner, tile_ids, queries, got] + turn
    specs = [smem, smem, hbm, hbm, vmem, vmem]
    if last:
        args += state + fresh
        specs += [hbm, hbm, hbm, hbm, vmem, vmem]
        rows = recompute * tile_len // sources
        part = all_rows // tile_len * head_dim
        out_shape = jax.ShapeDtypeStruct((sources, queries_dev, rows, part), queries.dtype)
        out_specs = vmem
        x, weights = fresh[:2]
        extra = [
            pltpu.VMEM(x.shape, x.dtype),
            pltpu.VMEM(weights.shape, weights.dtype),
            pltpu.VMEM((x.shape[0], weights.shape[1]), jnp.float32),
            pltpu.SemaphoreType.DMA((4, 2)),
        ]
    else:
        out_shape = [jax.ShapeDtypeStruct(shape, jnp.float32) for shape in shapes]
        out_specs = [hbm] * 2
        extra = []
    return pl.pallas_call(
        functools.partial(attend_kernel, exp_scale, tile_len, piece, pieces, last),
        in_specs=specs,
        out_specs=out_specs,
        out_shape=out_shape,
        scratch_shapes=[
            pltpu.VMEM(queries.shape, queries.dtype),
            pltpu.VMEM((queries_dev, slots) + got.shape[1:], got.dtype),
            pltpu.VMEM(shapes[0], jnp.float32),
            pltpu.VMEM(shapes[1], jnp.float32),
            pltpu.SemaphoreType.DMA((queries_dev,)),
            pltpu.SemaphoreType.DMA((queries_dev, slots)),
            pltpu.SemaphoreType.DMA((queries_dev, 2)),
        ]
        + extra,
        compiler_params=pltpu.CompilerParams(vmem_limit_bytes=(50 if last else 32) * 2**20),
        cost_estimate=pl.CostEstimate(
            flops=16 * 10**9 // pieces,
            bytes_accessed=12 * 10**6,
            transcendentals=16 * 10**6 // pieces,
        ),
        name="attend_last" if last else "attend_first",
    )(*args)


def body(
    tile_inputs,
    tile_queries,
    key_weight,
    value_weight,
    span_keys,
    span_values,
    span_slot,
    retrieval,
    tile_ids,
):
    queries_dev, tile_rows, width = tile_inputs.shape
    per_store, _, span_len, head_dim = span_keys.shape
    slot_count = retrieval.shape[1]
    recompute = tile_ids.shape[1]
    tile_len = tile_rows // recompute
    store_count = lax.axis_size("store")
    head_count = lax.axis_size("head")
    side = math.isqrt(store_count)
    exp_scale = head_dim ** (-0.5) * math.log2(math.e)

    store_rows = span_slot[retrieval]
    owners = store_rows // per_store
    hit = owners.reshape(1, -1) == jnp.arange(store_count, dtype=jnp.int32)[:, None]
    wanted = jnp.max(jnp.where(hit, (store_rows % per_store).reshape(1, -1), 0), axis=1)
    incoming = lax.all_to_all(
        wanted.reshape(store_count, 1), "store", split_axis=0, concat_axis=0, tiled=True
    )
    weights = lax.all_gather(
        jnp.concatenate([key_weight, value_weight], axis=1), "store", axis=0, tiled=True
    )
    pieces = 2
    picked = pick_spans(incoming.reshape(-1), span_keys, span_values, pieces)
    split = split_columns(tile_queries, head_count)
    ring = head_count // 2
    received = [split[0]]
    for step in range(1, head_count):
        pairs = [
            (me, 2 * ((me // 2 + step // 2) % ring) + (me + step) % 2) for me in range(head_count)
        ]
        received.append(lax.ppermute(split[step], "head", pairs))
    queries = assemble(received, recompute, head_dim)

    got = []
    for part in picked:
        if got:
            part, queries = lax.optimization_barrier((part, queries))
        got.append(lax.all_to_all(part, "store", split_axis=0, concat_axis=0, tiled=True))

    offsets = jnp.arange(tile_len, dtype=jnp.int32)
    positions = (tile_ids[:, :, None] * tile_len + offsets).reshape(-1)
    fresh_cos, fresh_sin = rope_tables(positions, head_dim)
    slot_cos, slot_sin = rope_tables(jnp.arange(slot_count, dtype=jnp.int32) * span_len, head_dim)

    fresh = [tile_inputs.reshape(queries_dev * tile_rows, width), weights, fresh_cos, fresh_sin]
    run = functools.partial(attend, owners, tile_ids, queries)
    turn = [slot_cos, slot_sin]
    state = run(got[0], turn, exp_scale, tile_len, head_count, 0, pieces)
    mixed = run(got[1], turn, exp_scale, tile_len, head_count, 1, pieces, list(state), fresh)
    return join_columns(
        lax.all_to_all(mixed, "head", split_axis=0, concat_axis=0, tiled=True)
    )


def solution(mesh):
    placed = (
        P("store", None, None),
        P("store", "head", None),
        P("store", "head"),
        P("store", "head"),
        P("store", "head", None, None),
        P("store", "head", None, None),
        P(),
        P("store", None),
        P("store", None),
    )
    return jax.shard_map(
        body, mesh=mesh, in_specs=placed, out_specs=P("store", "head", None), check_vma=False
    )
```

```python
import functools
import math

import jax
import jax.numpy as jnp
from jax import lax
from jax.experimental import pallas as pl
from jax.experimental.pallas import tpu as pltpu
from jax.sharding import PartitionSpec as P

rope_base = 1000000.0
low = -1e30


def rope_tables(positions, width):
    half_width = width // 2
    exponent = jnp.arange(half_width, dtype=jnp.float32) * (2.0 / width)
    frequency = jnp.power(jnp.float32(rope_base), -exponent)
    angle = positions.astype(jnp.float32)[..., None] * frequency
    cosine = jnp.cos(angle)
    sine = jnp.sin(angle)
    return (
        jnp.concatenate([cosine, cosine], axis=-1),
        jnp.concatenate([-sine, sine], axis=-1),
    )


def rotate(values, cosine, signed_sine):
    swapped = pltpu.roll(values, values.shape[-1] // 2, 1)
    return values * cosine + swapped * signed_sine


def whole(shape):
    return pl.BlockSpec(shape, lambda *_: (0,) * len(shape))


def head_partner(me, step, count, sign):
    ring = count // 2
    turn = lax.rem(me // 2 + sign * (step // 2) + ring, ring)
    return 2 * turn + lax.rem(lax.rem(me, 2) + lax.rem(step, 2), 2)


def split_kernel(x_ref, *o_refs):
    me = lax.axis_index("head")
    part = o_refs[0].shape[2]
    for step, o_ref in enumerate(o_refs):
        to = head_partner(me, step, len(o_refs), 1)
        o_ref[...] = x_ref[:, :, pl.ds(pl.multiple_of(to * part, part), part)]


def split_columns(x, pieces):
    lead, rows, width = x.shape
    out = jax.ShapeDtypeStruct((lead, rows, width // pieces), x.dtype)
    return pl.pallas_call(split_kernel, out_shape=[out] * pieces, name="split_columns")(x)


def assemble_kernel(*refs):
    pieces = refs[:-2]
    o_ref, staged = refs[-2:]
    me = lax.axis_index("head")
    for step, piece in enumerate(pieces):
        staged[head_partner(me, step, len(pieces), -1)] = piece[...]
    queries_dev, recompute, double, all_rows = o_ref.shape
    head_dim = double // 2
    sources, _, rows, part = staged.shape
    per_tile = sources // recompute
    tile_len = per_tile * rows
    marker = (lax.broadcasted_iota(jnp.int32, (head_dim, all_rows), 0) == 0).astype(jnp.bfloat16)
    for i in range(queries_dev):
        for j in range(recompute):
            tile = staged[j * per_tile : (j + 1) * per_tile, i].reshape(tile_len, part)
            for g in range(part // head_dim):
                o_ref[i, j, :head_dim, g * tile_len : (g + 1) * tile_len] = tile[
                    :, g * head_dim : (g + 1) * head_dim
                ].T
            o_ref[i, j, head_dim:, :] = marker


def assemble(pieces, recompute, head_dim):
    queries_dev, rows, part = pieces[0].shape
    all_rows = len(pieces) // recompute * rows * (part // head_dim)
    return pl.pallas_call(
        assemble_kernel,
        out_shape=jax.ShapeDtypeStruct((queries_dev, recompute, 2 * head_dim, all_rows), pieces[0].dtype),
        scratch_shapes=[pltpu.VMEM((len(pieces),) + pieces[0].shape, pieces[0].dtype)],
        compiler_params=pltpu.CompilerParams(vmem_limit_bytes=20 * 2**20),
        name="assemble",
    )(*pieces)


def join_kernel(*refs):
    pieces = refs[:-2]
    o_ref, sems = refs[-2:]
    me = lax.axis_index("head")
    part = pieces[0].shape[2]
    copies = []
    for step, piece in enumerate(pieces):
        at = head_partner(me, step, len(pieces), -1) * part
        copies.append(
            pltpu.make_async_copy(
                piece, o_ref.at[:, :, pl.ds(pl.multiple_of(at, part), part)], sems.at[step]
            )
        )
    for copy in copies:
        copy.start()
    for copy in copies:
        copy.wait()


def join_columns(pieces):
    lead, rows, part = pieces[0].shape
    return pl.pallas_call(
        join_kernel,
        in_specs=[pl.BlockSpec(memory_space=pltpu.VMEM)] * len(pieces),
        out_specs=pl.BlockSpec(memory_space=pltpu.HBM),
        out_shape=jax.ShapeDtypeStruct((lead, rows, len(pieces) * part), pieces[0].dtype),
        scratch_shapes=[pltpu.SemaphoreType.DMA((len(pieces),))],
        name="join_columns",
    )(*pieces)


def head_exchange(pieces):
    count = len(pieces)
    ring = count // 2
    received = [pieces[0]]
    for step in range(1, count):
        pairs = [(me, 2 * ((me // 2 + step // 2) % ring) + (me + step) % 2) for me in range(count)]
        received.append(lax.ppermute(pieces[step], "head", pairs))
    return received


def pick_kernel(rows_ref, keys_ref, values_ref, *o_refs):
    def step(d, carry):
        row = rows_ref[d]
        start = 0
        for o_ref in o_refs:
            at = slice(start, start + o_ref.shape[2])
            o_ref[d, 0] = keys_ref[row, 0, at]
            o_ref[d, 1] = values_ref[row, 0, at]
            start = at.stop
        return carry

    lax.fori_loop(0, o_refs[0].shape[0], step, 0)


def pick_spans(rows, keys, values, pieces):
    count = rows.shape[0]
    span_len, head_dim = keys.shape[2:]
    out = jax.ShapeDtypeStruct((count, 2, span_len // pieces, head_dim), keys.dtype)
    return pl.pallas_call(
        pick_kernel,
        in_specs=[
            pl.BlockSpec(memory_space=pltpu.SMEM),
            pl.BlockSpec(memory_space=pltpu.VMEM),
            pl.BlockSpec(memory_space=pltpu.VMEM),
        ],
        out_specs=[pl.BlockSpec(memory_space=pltpu.VMEM)] * pieces,
        out_shape=[out] * pieces,
        compiler_params=pltpu.CompilerParams(vmem_limit_bytes=20 * 2**20),
        name="pick_spans",
    )(rows, keys, values)


def blend(scores, before, exp_scale):
    after = jnp.maximum(before, jnp.max(scores, axis=0, keepdims=True))
    weights = jnp.exp2((scores - after) * exp_scale).astype(jnp.bfloat16)
    fade = jnp.exp2((before - after) * exp_scale)
    return after, weights, fade


def add_keys(exp_scale, q_ref, acc_ref, top_ref, where, keys, values, bias, wide):
    i, j = where
    all_rows = q_ref.shape[3]
    depth = keys.shape[1]
    ones = jnp.ones((acc_ref.shape[2] - values.shape[1], keys.shape[0]), jnp.bfloat16)
    values = jnp.concatenate([values.T, ones], axis=0)
    blocks = [pl.ds(start, wide) for start in range(0, all_rows, wide)]
    scores = {}
    tops = {}
    for turn in range(-1, len(blocks)):
        if turn + 1 < len(blocks):
            at = blocks[turn + 1]
            now = jnp.dot(keys, q_ref[i, j, :depth, at], preferred_element_type=jnp.float32)
            if bias is not None:
                now = now + bias
            scores[turn + 1] = now
            tops[turn + 1] = jnp.max(now, axis=0, keepdims=True)
        if turn >= 0:
            at = blocks[turn]
            before = top_ref[i, j, :1, at]
            after = jnp.maximum(before, tops.pop(turn))
            weights = jnp.exp2((scores.pop(turn) - after) * exp_scale).astype(jnp.bfloat16)
            fade = jnp.exp2((before - after) * exp_scale)
            top_ref[i, j, :1, at] = after
            acc_ref[i, j, :, at] = acc_ref[i, j, :, at] * fade + jnp.dot(
                values, weights, preferred_element_type=jnp.float32
            )


def attend_kernel(exp_scale, tile_len, piece, pieces, sources, last, *refs):
    refs = list(refs)
    owner_ref, tile_ref, q_ref, got_ref, cos_ref, sin_ref = refs[:6]
    del refs[:6]
    if last:
        state_ref, x_ref, w_ref, fresh_cos_ref, fresh_sin_ref = refs[:5]
        o_refs = refs[5 : 5 + sources]
        del refs[: 5 + sources]
    else:
        state_ref = refs.pop(0)
    q_all, held, acc_ref, top_ref, q_sems, span_sems, state_sems = refs[:7]
    if last:
        x_held, w_held, total, staged, x_sems = refs[7:]
    queries_dev, recompute, double, all_rows = q_all.shape
    slots, _, part_len, head_dim = held.shape[1:]
    wide = 4 * tile_len
    per_part = part_len // tile_len
    per_span = per_part * pieces

    def q_copy(i):
        return pltpu.make_async_copy(q_ref.at[i], q_all.at[i], q_sems.at[i])

    def span_copy(i, p):
        return pltpu.make_async_copy(
            got_ref.at[owner_ref[i, p]], held.at[i, p], span_sems.at[i, p]
        )

    def state_copies(i):
        kept = acc_ref.shape[2] - top_ref.shape[2]
        pairs = [
            (acc_ref.at[i, :, :kept], state_ref.at[i, :, :kept]),
            (top_ref.at[i], state_ref.at[i, :, kept:]),
        ]
        return [
            pltpu.make_async_copy(b, a, state_sems.at[i, k])
            if last
            else pltpu.make_async_copy(a, b, state_sems.at[i, k])
            for k, (a, b) in enumerate(pairs)
        ]

    for i in range(queries_dev):
        q_copy(i).start()
        for p in range(slots):
            span_copy(i, p).start()
        if last:
            for copy in state_copies(i):
                copy.start()
    if last:
        steps = x_sems.shape[0]
        depth = x_held.shape[1] // steps
        copies = []
        for s in range(steps):
            at = pl.ds(s * depth, depth)
            copies.append(pltpu.make_async_copy(x_ref.at[:, at], x_held.at[:, at], x_sems.at[s, 0]))
            copies.append(pltpu.make_async_copy(w_ref.at[at, :], w_held.at[at, :], x_sems.at[s, 1]))
        for copy in copies:
            copy.start()
    key_lane = lax.broadcasted_iota(jnp.int32, (part_len, head_dim), 1)
    key_row = lax.broadcasted_iota(jnp.int32, (part_len, head_dim), 0)
    for i in range(queries_dev):
        if last:
            for copy in state_copies(i):
                copy.wait()
        else:
            top_ref[i] = jnp.full(top_ref.shape[1:], low, jnp.float32)
            acc_ref[i] = jnp.zeros(acc_ref.shape[1:], jnp.float32)
        q_copy(i).wait()

        def step(n, carry, i=i):
            group = n // recompute
            j = lax.rem(n, recompute)
            own = tile_ref[i, j]
            other = tile_ref[i, recompute - 1 - j]

            @pl.when(j == 0)
            def _():
                for inner in range(pieces):
                    span_copy(i, group * pieces + inner).wait()

            needed = own - group * pieces * per_span - piece * per_part

            def add(count, i=i):
                key_parts = []
                value_parts = []
                for inner in range(count):
                    p = group * pieces + inner
                    turned = rotate(
                        held[i, p, 0].astype(jnp.float32),
                        cos_ref[pl.ds(p, 1), :],
                        sin_ref[pl.ds(p, 1), :],
                    ).astype(jnp.bfloat16)
                    key_tile = p * per_span + piece * per_part + key_row // tile_len
                    hidden = (key_lane == 0) & ((key_tile >= own) | (key_tile == other))
                    key_parts.append(
                        jnp.concatenate(
                            [turned, jnp.where(hidden, low, 0.0).astype(jnp.bfloat16)], axis=1
                        )
                    )
                    value_parts.append(held[i, p, 1])
                add_keys(
                    exp_scale,
                    q_all,
                    acc_ref,
                    top_ref,
                    (i, j),
                    jnp.concatenate(key_parts, axis=0),
                    jnp.concatenate(value_parts, axis=0),
                    None,
                    wide,
                )

            @pl.when((needed > 0) & (needed <= per_span))
            def _():
                add(1)

            @pl.when(needed > per_span)
            def _():
                add(2)

            return carry

        lax.fori_loop(0, slots // pieces * recompute, step, 0)
        if not last:
            for copy in state_copies(i):
                copy.start()
    if not last:
        for i in range(queries_dev):
            for copy in state_copies(i):
                copy.wait()
        return
    for copy in copies:
        copy.wait()
    total[...] = jnp.dot(x_held[:, :depth], w_held[:depth, :], preferred_element_type=jnp.float32)
    for s in range(1, steps):
        at = pl.ds(s * depth, depth)
        total[...] += jnp.dot(x_held[:, at], w_held[at, :], preferred_element_type=jnp.float32)
    fresh_keys = rotate(total[:, :head_dim], fresh_cos_ref[...], fresh_sin_ref[...]).astype(jnp.bfloat16)
    fresh_values = total[:, head_dim:].astype(jnp.bfloat16)
    rows = recompute * tile_len
    per_tile = sources // recompute
    key = lax.broadcasted_iota(jnp.int32, (rows, tile_len), 0)
    row = lax.broadcasted_iota(jnp.int32, (rows, tile_len), 1)
    for i in range(queries_dev):
        for j in range(recompute):
            own = tile_ref[i, j]
            other = tile_ref[i, recompute - 1 - j]
            in_own = key // tile_len == j
            allowed = (in_own & (key % tile_len <= row)) | (jnp.logical_not(in_own) & (other < own))
            bias = jnp.concatenate([jnp.where(allowed, 0.0, low)] * (wide // tile_len), axis=1)
            at_rows = slice(i * rows, (i + 1) * rows)
            add_keys(
                exp_scale, q_all, acc_ref, top_ref, (i, j), fresh_keys[at_rows], fresh_values[at_rows], bias, wide
            )
            for start in range(0, all_rows, wide):
                at = pl.ds(start, wide)
                result = acc_ref[i, j, :head_dim, at] * (1.0 / acc_ref[i, j, head_dim : head_dim + 1, at])
                result = result.astype(jnp.bfloat16).T
                for h in range(0, wide, tile_len):
                    column = (start + h) // tile_len * head_dim
                    staged[j * per_tile : (j + 1) * per_tile, i, :, column : column + head_dim] = result[
                        h : h + tile_len
                    ].reshape(per_tile, staged.shape[2], head_dim)
    me = lax.axis_index("head")
    for move, o_ref in enumerate(o_refs):
        o_ref[...] = staged[head_partner(me, move, sources, 1)]


def attend(owner, tile_ids, queries, got, turn, exp_scale, tile_len, sources, piece, pieces, state=None, fresh=None):
    queries_dev, recompute, double, all_rows = queries.shape
    head_dim = double // 2
    slots = owner.shape[1]
    last = state is not None
    vmem = pl.BlockSpec(memory_space=pltpu.VMEM)
    smem = pl.BlockSpec(memory_space=pltpu.SMEM)
    hbm = pl.BlockSpec(memory_space=pltpu.HBM)
    shapes = [
        (queries_dev, recompute, head_dim + 16, all_rows),
        (queries_dev, recompute, 8, all_rows),
    ]
    args = [owner, tile_ids, queries, got] + turn
    specs = [smem, smem, hbm, hbm, vmem, vmem]
    if last:
        args += [state] + fresh
        specs += [hbm, hbm, hbm, vmem, vmem]
        rows = recompute * tile_len // sources
        part = all_rows // tile_len * head_dim
        out_shape = [jax.ShapeDtypeStruct((queries_dev, rows, part), queries.dtype)] * sources
        out_specs = [vmem] * sources
        x, weights = fresh[:2]
        extra = [
            pltpu.VMEM(x.shape, x.dtype),
            pltpu.VMEM(weights.shape, weights.dtype),
            pltpu.VMEM((x.shape[0], weights.shape[1]), jnp.float32),
            pltpu.VMEM((sources, queries_dev, rows, part), queries.dtype),
            pltpu.SemaphoreType.DMA((4, 2)),
        ]
    else:
        out_shape = jax.ShapeDtypeStruct(shapes[0], jnp.float32)
        out_specs = hbm
        extra = []
    return pl.pallas_call(
        functools.partial(attend_kernel, exp_scale, tile_len, piece, pieces, sources, last),
        in_specs=specs,
        out_specs=out_specs,
        out_shape=out_shape,
        scratch_shapes=[
            pltpu.VMEM(queries.shape, queries.dtype),
            pltpu.VMEM((queries_dev, slots) + got.shape[1:], got.dtype),
            pltpu.VMEM(shapes[0], jnp.float32),
            pltpu.VMEM(shapes[1], jnp.float32),
            pltpu.SemaphoreType.DMA((queries_dev,)),
            pltpu.SemaphoreType.DMA((queries_dev, slots)),
            pltpu.SemaphoreType.DMA((queries_dev, 2)),
        ]
        + extra,
        compiler_params=pltpu.CompilerParams(vmem_limit_bytes=(50 if last else 32) * 2**20),
        cost_estimate=pl.CostEstimate(
            flops=16 * 10**9 // pieces,
            bytes_accessed=12 * 10**6,
            transcendentals=16 * 10**6 // pieces,
        ),
        name="attend_last" if last else "attend_first",
    )(*args)


def body(
    tile_inputs,
    tile_queries,
    key_weight,
    value_weight,
    span_keys,
    span_values,
    span_slot,
    retrieval,
    tile_ids,
):
    queries_dev, tile_rows, width = tile_inputs.shape
    per_store, _, span_len, head_dim = span_keys.shape
    slot_count = retrieval.shape[1]
    recompute = tile_ids.shape[1]
    tile_len = tile_rows // recompute
    store_count = lax.axis_size("store")
    head_count = lax.axis_size("head")
    side = math.isqrt(store_count)
    exp_scale = head_dim ** (-0.5) * math.log2(math.e)

    store_rows = span_slot[retrieval]
    owners = store_rows // per_store
    hit = owners.reshape(1, -1) == jnp.arange(store_count, dtype=jnp.int32)[:, None]
    wanted = jnp.max(jnp.where(hit, (store_rows % per_store).reshape(1, -1), 0), axis=1)
    incoming = lax.all_to_all(
        wanted.reshape(store_count, 1), "store", split_axis=0, concat_axis=0, tiled=True
    )
    weights = lax.all_gather(
        jnp.concatenate([key_weight, value_weight], axis=1), "store", axis=0, tiled=True
    )
    pieces = 2
    picked = pick_spans(incoming.reshape(-1), span_keys, span_values, pieces)
    split = split_columns(tile_queries, head_count)
    received = head_exchange(split)
    queries = assemble(received, recompute, head_dim)

    got = []
    for part in picked:
        if got:
            part, queries = lax.optimization_barrier((part, queries))
        got.append(lax.all_to_all(part, "store", split_axis=0, concat_axis=0, tiled=True))

    offsets = jnp.arange(tile_len, dtype=jnp.int32)
    positions = (tile_ids[:, :, None] * tile_len + offsets).reshape(-1)
    fresh_cos, fresh_sin = rope_tables(positions, head_dim)
    slot_cos, slot_sin = rope_tables(jnp.arange(slot_count, dtype=jnp.int32) * span_len, head_dim)

    fresh = [tile_inputs.reshape(queries_dev * tile_rows, width), weights, fresh_cos, fresh_sin]
    run = functools.partial(attend, owners, tile_ids, queries)
    turn = [slot_cos, slot_sin]
    state = run(got[0], turn, exp_scale, tile_len, head_count, 0, pieces)
    mixed = run(got[1], turn, exp_scale, tile_len, head_count, 1, pieces, state, fresh)
    return join_columns(head_exchange(mixed))


def solution(mesh):
    placed = (
        P("store", None, None),
        P("store", "head", None),
        P("store", "head"),
        P("store", "head"),
        P("store", "head", None, None),
        P("store", "head", None, None),
        P(),
        P("store", None),
        P("store", None),
    )
    return jax.shard_map(
        body, mesh=mesh, in_specs=placed, out_specs=P("store", "head", None), check_vma=False
    )
```

```python
import functools
import math

import jax
import jax.numpy as jnp
from jax import lax
from jax.experimental import pallas as pl
from jax.experimental.pallas import tpu as pltpu
from jax.sharding import PartitionSpec as P

rope_base = 1000000.0
low = -1e30


def rope_tables(positions, width):
    half_width = width // 2
    exponent = jnp.arange(half_width, dtype=jnp.float32) * (2.0 / width)
    frequency = jnp.power(jnp.float32(rope_base), -exponent)
    angle = positions.astype(jnp.float32)[..., None] * frequency
    cosine = jnp.cos(angle)
    sine = jnp.sin(angle)
    return (
        jnp.concatenate([cosine, cosine], axis=-1),
        jnp.concatenate([-sine, sine], axis=-1),
    )


def rotate(values, cosine, signed_sine):
    swapped = pltpu.roll(values, values.shape[-1] // 2, 1)
    return values * cosine + swapped * signed_sine


def whole(shape):
    return pl.BlockSpec(shape, lambda *_: (0,) * len(shape))


def head_partner(me, step, count, sign):
    ring = count // 2
    turn = lax.rem(me // 2 + sign * (step // 2) + ring, ring)
    return 2 * turn + lax.rem(lax.rem(me, 2) + lax.rem(step, 2), 2)


def split_kernel(x_ref, *o_refs):
    me = lax.axis_index("head")
    part = o_refs[0].shape[2]
    for step, o_ref in enumerate(o_refs):
        to = head_partner(me, step, len(o_refs), 1)
        o_ref[...] = x_ref[:, :, pl.ds(pl.multiple_of(to * part, part), part)]


def split_columns(x, pieces):
    lead, rows, width = x.shape
    out = jax.ShapeDtypeStruct((lead, rows, width // pieces), x.dtype)
    return pl.pallas_call(split_kernel, out_shape=[out] * pieces, compiler_params=pltpu.CompilerParams(vmem_limit_bytes=8 * 2**20), name="split_columns")(x)


def assemble_kernel(*refs):
    pieces = refs[:-2]
    o_ref, staged = refs[-2:]
    me = lax.axis_index("head")
    for step, piece in enumerate(pieces):
        staged[head_partner(me, step, len(pieces), -1)] = piece[...]
    queries_dev, recompute, double, all_rows = o_ref.shape
    head_dim = double // 2
    sources, _, rows, part = staged.shape
    per_tile = sources // recompute
    tile_len = per_tile * rows
    marker = (lax.broadcasted_iota(jnp.int32, (head_dim, all_rows), 0) == 0).astype(jnp.bfloat16)
    for i in range(queries_dev):
        for j in range(recompute):
            tile = staged[j * per_tile : (j + 1) * per_tile, i].reshape(tile_len, part)
            for g in range(part // head_dim):
                o_ref[i, j, :head_dim, g * tile_len : (g + 1) * tile_len] = tile[
                    :, g * head_dim : (g + 1) * head_dim
                ].T
            o_ref[i, j, head_dim:, :] = marker


def assemble(pieces, recompute, head_dim):
    queries_dev, rows, part = pieces[0].shape
    all_rows = len(pieces) // recompute * rows * (part // head_dim)
    return pl.pallas_call(
        assemble_kernel,
        out_shape=jax.ShapeDtypeStruct((queries_dev, recompute, 2 * head_dim, all_rows), pieces[0].dtype),
        scratch_shapes=[pltpu.VMEM((len(pieces),) + pieces[0].shape, pieces[0].dtype)],
        compiler_params=pltpu.CompilerParams(vmem_limit_bytes=20 * 2**20),
        name="assemble",
    )(*pieces)


def join_kernel(*refs):
    pieces = refs[:-2]
    o_ref, sems = refs[-2:]
    me = lax.axis_index("head")
    part = pieces[0].shape[2]
    copies = []
    for step, piece in enumerate(pieces):
        at = head_partner(me, step, len(pieces), -1) * part
        copies.append(
            pltpu.make_async_copy(
                piece, o_ref.at[:, :, pl.ds(pl.multiple_of(at, part), part)], sems.at[step]
            )
        )
    for copy in copies:
        copy.start()
    for copy in copies:
        copy.wait()


def join_columns(pieces):
    lead, rows, part = pieces[0].shape
    return pl.pallas_call(
        join_kernel,
        in_specs=[pl.BlockSpec(memory_space=pltpu.VMEM)] * len(pieces),
        out_specs=pl.BlockSpec(memory_space=pltpu.HBM),
        out_shape=jax.ShapeDtypeStruct((lead, rows, len(pieces) * part), pieces[0].dtype),
        scratch_shapes=[pltpu.SemaphoreType.DMA((len(pieces),))],
        compiler_params=pltpu.CompilerParams(vmem_limit_bytes=8 * 2**20),
        name="join_columns",
    )(*pieces)


def head_exchange(pieces):
    count = len(pieces)
    ring = count // 2
    received = [pieces[0]]
    for step in range(1, count):
        pairs = [(me, 2 * ((me // 2 + step // 2) % ring) + (me + step) % 2) for me in range(count)]
        received.append(lax.ppermute(pieces[step], "head", pairs))
    return received


def pick_kernel(start, rows_ref, keys_ref, values_ref, o_ref):
    at = slice(start, start + o_ref.shape[2])

    def step(d, carry):
        row = rows_ref[d]
        o_ref[d, 0] = keys_ref[row, 0, at]
        o_ref[d, 1] = values_ref[row, 0, at]
        return carry

    lax.fori_loop(0, o_ref.shape[0], step, 0)


def pick_spans(rows, keys, values, piece, pieces):
    count = rows.shape[0]
    span_len, head_dim = keys.shape[2:]
    part = span_len // pieces
    vmem = pl.BlockSpec(memory_space=pltpu.VMEM)
    return pl.pallas_call(
        functools.partial(pick_kernel, piece * part),
        in_specs=[pl.BlockSpec(memory_space=pltpu.SMEM), vmem, vmem],
        out_specs=vmem,
        out_shape=jax.ShapeDtypeStruct((count, 2, part, head_dim), keys.dtype),
        compiler_params=pltpu.CompilerParams(vmem_limit_bytes=20 * 2**20),
        name="pick_spans",
    )(rows, keys, values)


def blend(scores, before, exp_scale):
    after = jnp.maximum(before, jnp.max(scores, axis=0, keepdims=True))
    weights = jnp.exp2((scores - after) * exp_scale).astype(jnp.bfloat16)
    fade = jnp.exp2((before - after) * exp_scale)
    return after, weights, fade


def add_keys(exp_scale, q_ref, acc_ref, top_ref, where, keys, values, bias, wide):
    i, j = where
    all_rows = q_ref.shape[3]
    depth = keys.shape[1]
    ones = jnp.ones((acc_ref.shape[2] - values.shape[1], keys.shape[0]), jnp.bfloat16)
    values = jnp.concatenate([values.T, ones], axis=0)
    blocks = [pl.ds(start, wide) for start in range(0, all_rows, wide)]
    scores = {}
    tops = {}
    for turn in range(-1, len(blocks)):
        if turn + 1 < len(blocks):
            at = blocks[turn + 1]
            now = jnp.dot(keys, q_ref[i, j, :depth, at], preferred_element_type=jnp.float32)
            if bias is not None:
                now = now + bias
            scores[turn + 1] = now
            tops[turn + 1] = jnp.max(now, axis=0, keepdims=True)
        if turn >= 0:
            at = blocks[turn]
            before = top_ref[i, j, :1, at]
            after = jnp.maximum(before, tops.pop(turn))
            weights = jnp.exp2((scores.pop(turn) - after) * exp_scale).astype(jnp.bfloat16)
            fade = jnp.exp2((before - after) * exp_scale)
            top_ref[i, j, :1, at] = after
            acc_ref[i, j, :, at] = acc_ref[i, j, :, at] * fade + jnp.dot(
                values, weights, preferred_element_type=jnp.float32
            )


def attend_kernel(exp_scale, tile_len, piece, pieces, sources, last, *refs):
    refs = list(refs)
    owner_ref, tile_ref, q_ref, got_ref, cos_ref, sin_ref = refs[:6]
    del refs[:6]
    if last:
        state_ref, x_ref, w_ref, fresh_cos_ref, fresh_sin_ref = refs[:5]
        o_refs = refs[5 : 5 + sources]
        del refs[: 5 + sources]
    else:
        state_ref = refs.pop(0)
    q_all, held, acc_ref, top_ref, q_sems, span_sems, state_sems = refs[:7]
    if last:
        x_held, w_held, total, staged, x_sems = refs[7:]
    queries_dev, recompute, double, all_rows = q_all.shape
    slots, _, part_len, head_dim = held.shape[1:]
    wide = 4 * tile_len
    per_part = part_len // tile_len
    per_span = per_part * pieces

    def q_copy(i):
        return pltpu.make_async_copy(q_ref.at[i], q_all.at[i], q_sems.at[i])

    def span_copy(i, p):
        return pltpu.make_async_copy(
            got_ref.at[owner_ref[i, p]], held.at[i, p], span_sems.at[i, p]
        )

    def state_copies(i):
        kept = acc_ref.shape[2] - top_ref.shape[2]
        pairs = [
            (acc_ref.at[i, :, :kept], state_ref.at[i, :, :kept]),
            (top_ref.at[i], state_ref.at[i, :, kept:]),
        ]
        return [
            pltpu.make_async_copy(b, a, state_sems.at[i, k])
            if last
            else pltpu.make_async_copy(a, b, state_sems.at[i, k])
            for k, (a, b) in enumerate(pairs)
        ]

    for i in range(queries_dev):
        q_copy(i).start()
        for p in range(slots):
            span_copy(i, p).start()
        if last:
            for copy in state_copies(i):
                copy.start()
    if last:
        steps = x_sems.shape[0]
        depth = x_held.shape[1] // steps
        copies = []
        for s in range(steps):
            at = pl.ds(s * depth, depth)
            copies.append(pltpu.make_async_copy(x_ref.at[:, at], x_held.at[:, at], x_sems.at[s, 0]))
            copies.append(pltpu.make_async_copy(w_ref.at[at, :], w_held.at[at, :], x_sems.at[s, 1]))
        for copy in copies:
            copy.start()
    key_lane = lax.broadcasted_iota(jnp.int32, (part_len, head_dim), 1)
    key_row = lax.broadcasted_iota(jnp.int32, (part_len, head_dim), 0)
    for i in range(queries_dev):
        if last:
            for copy in state_copies(i):
                copy.wait()
        else:
            top_ref[i] = jnp.full(top_ref.shape[1:], low, jnp.float32)
            acc_ref[i] = jnp.zeros(acc_ref.shape[1:], jnp.float32)
        q_copy(i).wait()

        def step(n, carry, i=i):
            group = n // recompute
            j = lax.rem(n, recompute)
            own = tile_ref[i, j]
            other = tile_ref[i, recompute - 1 - j]

            @pl.when(j == 0)
            def _():
                for inner in range(pieces):
                    span_copy(i, group * pieces + inner).wait()

            needed = own - group * pieces * per_span - piece * per_part

            def add(count, i=i):
                key_parts = []
                value_parts = []
                for inner in range(count):
                    p = group * pieces + inner
                    turned = rotate(
                        held[i, p, 0].astype(jnp.float32),
                        cos_ref[pl.ds(p, 1), :],
                        sin_ref[pl.ds(p, 1), :],
                    ).astype(jnp.bfloat16)
                    key_tile = p * per_span + piece * per_part + key_row // tile_len
                    hidden = (key_lane == 0) & ((key_tile >= own) | (key_tile == other))
                    key_parts.append(
                        jnp.concatenate(
                            [turned, jnp.where(hidden, low, 0.0).astype(jnp.bfloat16)], axis=1
                        )
                    )
                    value_parts.append(held[i, p, 1])
                add_keys(
                    exp_scale,
                    q_all,
                    acc_ref,
                    top_ref,
                    (i, j),
                    jnp.concatenate(key_parts, axis=0),
                    jnp.concatenate(value_parts, axis=0),
                    None,
                    wide,
                )

            @pl.when((needed > 0) & (needed <= per_span))
            def _():
                add(1)

            @pl.when(needed > per_span)
            def _():
                add(2)

            return carry

        lax.fori_loop(0, slots // pieces * recompute, step, 0)
        if not last:
            for copy in state_copies(i):
                copy.start()
    if not last:
        for i in range(queries_dev):
            for copy in state_copies(i):
                copy.wait()
        return
    for copy in copies:
        copy.wait()
    total[...] = jnp.dot(x_held[:, :depth], w_held[:depth, :], preferred_element_type=jnp.float32)
    for s in range(1, steps):
        at = pl.ds(s * depth, depth)
        total[...] += jnp.dot(x_held[:, at], w_held[at, :], preferred_element_type=jnp.float32)
    fresh_keys = rotate(total[:, :head_dim], fresh_cos_ref[...], fresh_sin_ref[...]).astype(jnp.bfloat16)
    fresh_values = total[:, head_dim:].astype(jnp.bfloat16)
    rows = recompute * tile_len
    per_tile = sources // recompute
    key = lax.broadcasted_iota(jnp.int32, (rows, tile_len), 0)
    row = lax.broadcasted_iota(jnp.int32, (rows, tile_len), 1)
    for i in range(queries_dev):
        for j in range(recompute):
            own = tile_ref[i, j]
            other = tile_ref[i, recompute - 1 - j]
            in_own = key // tile_len == j
            allowed = (in_own & (key % tile_len <= row)) | (jnp.logical_not(in_own) & (other < own))
            bias = jnp.concatenate([jnp.where(allowed, 0.0, low)] * (wide // tile_len), axis=1)
            at_rows = slice(i * rows, (i + 1) * rows)
            add_keys(
                exp_scale, q_all, acc_ref, top_ref, (i, j), fresh_keys[at_rows], fresh_values[at_rows], bias, wide
            )
            for start in range(0, all_rows, wide):
                at = pl.ds(start, wide)
                result = acc_ref[i, j, :head_dim, at] * (1.0 / acc_ref[i, j, head_dim : head_dim + 1, at])
                result = result.astype(jnp.bfloat16).T
                for h in range(0, wide, tile_len):
                    column = (start + h) // tile_len * head_dim
                    staged[j * per_tile : (j + 1) * per_tile, i, :, column : column + head_dim] = result[
                        h : h + tile_len
                    ].reshape(per_tile, staged.shape[2], head_dim)
    me = lax.axis_index("head")
    for move, o_ref in enumerate(o_refs):
        o_ref[...] = staged[head_partner(me, move, sources, 1)]


def attend(owner, tile_ids, queries, got, turn, exp_scale, tile_len, sources, piece, pieces, state=None, fresh=None):
    queries_dev, recompute, double, all_rows = queries.shape
    head_dim = double // 2
    slots = owner.shape[1]
    last = state is not None
    vmem = pl.BlockSpec(memory_space=pltpu.VMEM)
    smem = pl.BlockSpec(memory_space=pltpu.SMEM)
    hbm = pl.BlockSpec(memory_space=pltpu.HBM)
    shapes = [
        (queries_dev, recompute, head_dim + 16, all_rows),
        (queries_dev, recompute, 8, all_rows),
    ]
    args = [owner, tile_ids, queries, got] + turn
    specs = [smem, smem, hbm, hbm, vmem, vmem]
    if last:
        args += [state] + fresh
        specs += [hbm, hbm, hbm, vmem, vmem]
        rows = recompute * tile_len // sources
        part = all_rows // tile_len * head_dim
        out_shape = [jax.ShapeDtypeStruct((queries_dev, rows, part), queries.dtype)] * sources
        out_specs = [vmem] * sources
        x, weights = fresh[:2]
        extra = [
            pltpu.VMEM(x.shape, x.dtype),
            pltpu.VMEM(weights.shape, weights.dtype),
            pltpu.VMEM((x.shape[0], weights.shape[1]), jnp.float32),
            pltpu.VMEM((sources, queries_dev, rows, part), queries.dtype),
            pltpu.SemaphoreType.DMA((4, 2)),
        ]
    else:
        out_shape = jax.ShapeDtypeStruct(shapes[0], jnp.float32)
        out_specs = hbm
        extra = []
    return pl.pallas_call(
        functools.partial(attend_kernel, exp_scale, tile_len, piece, pieces, sources, last),
        in_specs=specs,
        out_specs=out_specs,
        out_shape=out_shape,
        scratch_shapes=[
            pltpu.VMEM(queries.shape, queries.dtype),
            pltpu.VMEM((queries_dev, slots) + got.shape[1:], got.dtype),
            pltpu.VMEM(shapes[0], jnp.float32),
            pltpu.VMEM(shapes[1], jnp.float32),
            pltpu.SemaphoreType.DMA((queries_dev,)),
            pltpu.SemaphoreType.DMA((queries_dev, slots)),
            pltpu.SemaphoreType.DMA((queries_dev, 2)),
        ]
        + extra,
        compiler_params=pltpu.CompilerParams(vmem_limit_bytes=(50 if last else 32) * 2**20),
        cost_estimate=pl.CostEstimate(
            flops=16 * 10**9 // pieces,
            bytes_accessed=12 * 10**6,
            transcendentals=16 * 10**6 // pieces,
        ),
        name="attend_last" if last else "attend_first",
    )(*args)


def body(
    tile_inputs,
    tile_queries,
    key_weight,
    value_weight,
    span_keys,
    span_values,
    span_slot,
    retrieval,
    tile_ids,
):
    queries_dev, tile_rows, width = tile_inputs.shape
    per_store, _, span_len, head_dim = span_keys.shape
    slot_count = retrieval.shape[1]
    recompute = tile_ids.shape[1]
    tile_len = tile_rows // recompute
    store_count = lax.axis_size("store")
    head_count = lax.axis_size("head")
    side = math.isqrt(store_count)
    exp_scale = head_dim ** (-0.5) * math.log2(math.e)

    store_rows = span_slot[retrieval]
    owners = store_rows // per_store
    hit = owners.reshape(1, -1) == jnp.arange(store_count, dtype=jnp.int32)[:, None]
    wanted = jnp.max(jnp.where(hit, (store_rows % per_store).reshape(1, -1), 0), axis=1)
    incoming = lax.all_to_all(
        wanted.reshape(store_count, 1), "store", split_axis=0, concat_axis=0, tiled=True
    )
    weights = lax.all_gather(
        jnp.concatenate([key_weight, value_weight], axis=1), "store", axis=0, tiled=True
    )
    pieces = 2
    rows = incoming.reshape(-1)
    split = split_columns(tile_queries, head_count)
    received = head_exchange(split)
    queries = assemble(received, recompute, head_dim)

    got = []
    for piece in range(pieces):
        if got:
            rows, queries = lax.optimization_barrier((rows, queries))
        got.append(
            lax.all_to_all(
                pick_spans(rows, span_keys, span_values, piece, pieces),
                "store",
                split_axis=0,
                concat_axis=0,
                tiled=True,
            )
        )

    offsets = jnp.arange(tile_len, dtype=jnp.int32)
    positions = (tile_ids[:, :, None] * tile_len + offsets).reshape(-1)
    fresh_cos, fresh_sin = rope_tables(positions, head_dim)
    slot_cos, slot_sin = rope_tables(jnp.arange(slot_count, dtype=jnp.int32) * span_len, head_dim)

    fresh = [tile_inputs.reshape(queries_dev * tile_rows, width), weights, fresh_cos, fresh_sin]
    run = functools.partial(attend, owners, tile_ids, queries)
    turn = [slot_cos, slot_sin]
    state = run(got[0], turn, exp_scale, tile_len, head_count, 0, pieces)
    mixed = run(got[1], turn, exp_scale, tile_len, head_count, 1, pieces, state, fresh)
    return join_columns(head_exchange(mixed))


def solution(mesh):
    placed = (
        P("store", None, None),
        P("store", "head", None),
        P("store", "head"),
        P("store", "head"),
        P("store", "head", None, None),
        P("store", "head", None, None),
        P(),
        P("store", None),
        P("store", None),
    )
    return jax.shard_map(
        body, mesh=mesh, in_specs=placed, out_specs=P("store", "head", None), check_vma=False
    )
```
